512 devices in a mesh: dp: 128 (over z, y, core), mp: 4 (over x).
Axes of the slice: x: 4, y: 8, z: 8, core: 2. Of those that a mesh axis runs over, the one named last changes fastest.
Arguments:
- tokens: bfloat16 [16384, 8192], P('dp', 'mp'), may hold values from -6 to 6
- fixed_value_weight: bfloat16 [8192, 1024], P('mp', 'dp'), may hold values from -0.0625 to 0.0625
- output_gradient: bfloat16 [16384, 1024], P('dp', 'mp'), may hold values from -6 to 6
- adapter_down_factor: bfloat16 [128, 8192, 64], P('dp', 'mp'), may hold values from -0.0625 to 0.0625
- adapter_up_factor: bfloat16 [128, 64, 1024], P('dp', None, 'mp'), may hold values from -0.75 to 0.75
- adapter_per_token: int32 [16384, 1], P('dp'), may hold values from 0 to 127; in each aligned block of 128 rows (0 to 127, 128 to 255, ...) at most 2 rows name the same one
- adapter_owner_index: int32 [128], replicated, may hold values from 0 to 127, each once
Outputs:
- projected: bfloat16 [16384, 1024], P('dp', 'mp')
- activation_gradient: bfloat16 [16384, 8192], P('dp', 'mp')
- down_factor_gradient: float32 [128, 8192, 64], P('dp', 'mp')
- up_factor_gradient: float32 [128, 64, 1024], P('dp', None, 'mp')
The draws below stay inside these ranges and needn't reach their ends.
Inputs may be any that keep to these rules, and one draw needn't show every extreme that they name: `adapter_per_token`: among the tokens of one index of dp no adapter is named more than 2 times, and in some indices one is named exactly 2 times; every adapter is named by some token. `adapter_owner_index`: every owner index is named by exactly one adapter.
All inputs are finite; a program needn't handle non-finite values.
Results may differ from the reference program's by a relative error of at most 0.0037.
Values may be sent and summed in bfloat16 or wider, within the bound.
No kernel may reach another device: no remote copies, remote signals or barrier semaphores. Data moves between devices by JAX's collectives and lax.ppermute only.
A program may use at most 64 MiB of HBM per device.

```python
import math
import jax
import jax.numpy as jnp
import numpy as np
from jax import lax

MODEL_WIDTH = 8192
ADAPTER_RANK = 64
TOK_DEV = 128
VALUE_FEATURES = 1024
ADAPTER_COUNT = 128
CAP = 2
TOKENS = 16384
N_DP = 128


def block_levels(own_key, extent, pieces, least, high):
    level, own = 1.0, jax.random.fold_in(own_key, 6)
    for axis_at, shards_of in pieces:
        steps = jnp.exp(jax.random.uniform(jax.random.fold_in(own, axis_at), (shards_of,), jnp.float32, least / len(pieces), high / len(pieces)))
        level = level * jnp.repeat(steps, extent[axis_at] // shards_of).reshape([-1 if axis == axis_at else 1 for axis in range(len(extent))])
    return level


def shared_out(stream_key, own, number, rows, number_of, top, bound, skew):
    order = jax.random.permutation(stream_key, number_of)
    heavy_load, ordinary = load_shares(number_of, rows * top, bound, skew, True), load_shares(number_of, rows * top, bound, skew, False)
    places = jnp.arange(number_of)

    def named(lengths, rotation):
        used = int((lengths > 0).sum())
        fixed = max(1, used // 4)
        shifted = fixed + (places - fixed + rotation * (used - fixed)) % max(1, number_of - fixed)
        return jnp.zeros((number_of,), jnp.int32).at[order[jnp.where(places < fixed, places, shifted)]].set(jnp.asarray(lengths, jnp.int32))

    lengths = jnp.where(number % 4 == 0, named(heavy_load, number // 4), named(ordinary, number - number // 4 - 1))
    mixed = jax.random.permutation(jax.random.fold_in(own, 3), number_of)
    giver, receiver = mixed[0:number_of // 2 * 2:2], mixed[1:number_of // 2 * 2:2]
    margin = jnp.minimum(lengths[giver] - 1, bound - lengths[receiver]) // 2
    margin = jnp.where((giver == order[0]) | (receiver == order[0]) | (lengths[receiver] == 0), 0, jnp.maximum(margin, 0))
    shifted = jax.random.randint(jax.random.fold_in(own, 4), (number_of // 2,), 0, 1 << 20) % (margin + 1)
    lengths = lengths.at[giver].add(-shifted).at[receiver].add(shifted)
    items = jnp.searchsorted(jnp.cumsum(lengths), jnp.arange(rows * top), side="right").astype(jnp.int32)
    grid = items.reshape(top, rows).T
    grid = grid[jax.random.permutation(jax.random.fold_in(own, 1), rows)]
    rotation = jax.random.randint(jax.random.fold_in(own, 2), (rows, 1), 0, top)
    return jnp.take_along_axis(grid, (jnp.arange(top)[None, :] + rotation) % top, axis=1)


def load_shares(number_of, total, bound, skew, full):
    portions = [(1 << 20) // math.isqrt(rank ** skew) + 1 for rank in range(1, number_of + 1)]
    largest = bound if full else min(bound, max(-(-total // number_of), total * portions[0] // sum(portions)))
    least = 1 if total - largest >= number_of - 1 else 0
    given, spare = [largest] + [least] * (number_of - 1), total - largest - least * (number_of - 1)
    while spare > 0:
        candidates = [i for i in range(1, number_of) if given[i] < largest] or [i for i in range(1, number_of) if given[i] < bound]
        whole, budget = sum([portions[i] for i in candidates]), spare
        for i in candidates:
            more = min(bound - given[i], max(1, budget * portions[i] // whole), spare)
            given[i] = given[i] + more
            spare = spare - more
    return np.array(given)


def bell_draw(rng, dims, scale, limit, split=(), kind=jnp.bfloat16):
    array = scale * jax.random.normal(rng, dims, jnp.float32)
    if split:
        array = array * block_levels(rng, dims, split, -0.22, 0.18)
    return jnp.clip(array, -limit, limit).astype(kind)


def setup_inputs(seed: int = 0) -> dict:
    seeds = jax.random.split(jax.random.key(seed), 8)
    tokens = bell_draw(seeds[0], (TOKENS, MODEL_WIDTH), 1.0, 6.0, ((0, 128), (1, 4)))
    fixed_value_weight = bell_draw(seeds[1], (MODEL_WIDTH, VALUE_FEATURES), MODEL_WIDTH ** -0.5, 0.0625, ((0, 4), (1, 128)))
    output_gradient = bell_draw(seeds[2], (TOKENS, VALUE_FEATURES), 1.0, 6.0, ((0, 128), (1, 4)))
    adapter_down_factor = bell_draw(seeds[3], (ADAPTER_COUNT, MODEL_WIDTH, ADAPTER_RANK), MODEL_WIDTH ** -0.5, 0.0625, ((0, 128), (1, 4)))
    adapter_up_factor = bell_draw(seeds[4], (ADAPTER_COUNT, ADAPTER_RANK, VALUE_FEATURES), ADAPTER_RANK ** -0.5, 0.75, ((0, 128), (2, 4)))
    adapter_per_token_keys = jax.random.split(jax.random.fold_in(seeds[5], 1), TOKENS // TOK_DEV)
    adapter_per_token_turns = jax.random.permutation(jax.random.fold_in(seeds[5], 3), TOKENS // TOK_DEV)
    adapter_per_token = jax.vmap(lambda own, number: shared_out(jax.random.fold_in(seeds[5], 2), own, number, TOK_DEV, ADAPTER_COUNT, 1, CAP, 2))(adapter_per_token_keys, adapter_per_token_turns).reshape((TOKENS, 1))
    adapter_owner_index = jax.random.permutation(seeds[6], N_DP).astype(jnp.int32)
    return dict(tokens=tokens, fixed_value_weight=fixed_value_weight, output_gradient=output_gradient, adapter_down_factor=adapter_down_factor, adapter_up_factor=adapter_up_factor, adapter_per_token=adapter_per_token, adapter_owner_index=adapter_owner_index)


adapter_scale = 0.5


def owner_slots(adapter_per_token, adapter_owner_index):
    matches_adapter = adapter_per_token == jnp.arange(ADAPTER_COUNT, dtype=jnp.int32)[None, :]
    targets = jnp.sum(jnp.where(matches_adapter, adapter_owner_index[None, :], 0), axis=1).astype(jnp.int32)
    grouped = targets.reshape(N_DP, TOK_DEV)
    matches = (grouped[:, :, None] == jnp.arange(N_DP, dtype=jnp.int32)[None, None, :]).astype(jnp.int32)
    before = jnp.cumsum(matches, axis=1) - matches
    places = jnp.sum(before * matches, axis=2).astype(jnp.int32)
    sources = jnp.broadcast_to(jnp.arange(N_DP, dtype=jnp.int32)[:, None], (N_DP, TOK_DEV))
    token_index = jnp.arange(TOKENS, dtype=jnp.int32).reshape(N_DP, TOK_DEV)
    lookup_matrix = jnp.full((N_DP, N_DP, CAP), -1, jnp.int32).at[grouped, sources, places].set(token_index)
    return lookup_matrix.reshape(N_DP, N_DP * CAP)


def reference(tokens, fixed_value_weight, output_gradient, adapter_down_factor, adapter_up_factor, adapter_per_token, adapter_owner_index):
    lookup_matrix = owner_slots(adapter_per_token, adapter_owner_index)

    def visit_owner(loop_state, inputs):
        adapter_output, adapter_input = loop_state
        indices, down_matrix, upper_matrix = inputs
        valid = indices >= 0
        safe = jnp.maximum(indices, 0)
        picked_rows = jnp.where(valid[:, None], tokens[safe], jnp.zeros((), tokens.dtype))
        picked_gradient = jnp.where(valid[:, None], output_gradient[safe], jnp.zeros((), output_gradient.dtype))
        hidden_state = jnp.dot(picked_rows, down_matrix, preferred_element_type=jnp.float32).astype(jnp.bfloat16)
        message_rows = jnp.dot(picked_gradient, upper_matrix.T, preferred_element_type=jnp.float32).astype(jnp.bfloat16)
        extra_output = (adapter_scale * jnp.dot(hidden_state, upper_matrix, preferred_element_type=jnp.float32)).astype(jnp.bfloat16)
        extra_input = (adapter_scale * jnp.dot(message_rows, down_matrix.T, preferred_element_type=jnp.float32)).astype(jnp.bfloat16)
        down_factor_gradient = adapter_scale * jnp.dot(picked_rows.T, message_rows, preferred_element_type=jnp.float32)
        up_factor_gradient = adapter_scale * jnp.dot(hidden_state.T, picked_gradient, preferred_element_type=jnp.float32)
        destination = jnp.where(valid, indices, TOKENS).astype(jnp.int32)
        adapter_output = adapter_output.at[destination].set(extra_output.astype(adapter_output.dtype), mode="drop")
        adapter_input = adapter_input.at[destination].set(extra_input.astype(adapter_input.dtype), mode="drop")
        return (adapter_output, adapter_input), (down_factor_gradient, up_factor_gradient)

    start_offset = (jnp.zeros((TOKENS, VALUE_FEATURES), jnp.bfloat16), jnp.zeros((TOKENS, MODEL_WIDTH), jnp.bfloat16))
    (adapter_output, adapter_input), (down_gradient_list, up_gradient_list) = lax.scan(visit_owner, start_offset, (lookup_matrix, adapter_down_factor, adapter_up_factor))
    plain_output = jnp.dot(tokens, fixed_value_weight, preferred_element_type=jnp.float32)
    projected = (plain_output + adapter_output.astype(jnp.float32)).astype(jnp.bfloat16)
    plain_input = jnp.dot(output_gradient, fixed_value_weight.T, preferred_element_type=jnp.float32)
    activation_gradient = (plain_input + adapter_input.astype(jnp.float32)).astype(jnp.bfloat16)
    return (projected, activation_gradient, down_gradient_list, up_gradient_list)
```

```python
import jax
import jax.numpy as jnp
from jax import lax
from jax.sharding import PartitionSpec as P

adapter_scale = 0.5
f32 = jnp.float32
bf16 = jnp.bfloat16


def dot(left, right, contract):
    return lax.dot_general(left, right, ((contract[0], contract[1]), ((), ())), preferred_element_type=f32)


def slot_matrix(adapter_per_token, adapter_owner_index, owners, capacity):
    token_count = adapter_per_token.shape[0]
    adapters = adapter_owner_index.shape[0]
    adapter_of = adapter_per_token.reshape(1, token_count)
    names = (adapter_of == lax.broadcasted_iota(jnp.int32, (adapters, token_count), 0)).astype(bf16)
    owned = (
        adapter_owner_index[None, :] == lax.broadcasted_iota(jnp.int32, (owners, adapters), 0)
    ).astype(bf16)
    matches = dot(owned, names, ((1,), (0,)))
    earlier = (
        lax.broadcasted_iota(jnp.int32, (token_count, token_count), 0)
        < lax.broadcasted_iota(jnp.int32, (token_count, token_count), 1)
    ).astype(bf16)
    before = dot(matches.astype(bf16), earlier, ((1,), (0,)))
    place = jnp.arange(capacity, dtype=f32)[None, :, None]
    picks = jnp.where(before[:, None, :] == place, matches[:, None, :], 0.0).astype(bf16)
    return picks.reshape(owners * capacity, token_count)


def body(
    tokens,
    fixed_value_weight,
    output_gradient,
    adapter_down_factor,
    adapter_up_factor,
    adapter_per_token,
    adapter_owner_index,
):
    owners = lax.axis_size("dp")
    parts = lax.axis_size("mp")
    token_count, width = tokens.shape
    features = output_gradient.shape[1]
    rank = adapter_down_factor.shape[2]
    capacity = max(2, 2 * token_count // owners)
    slots = owners * capacity
    down_matrix = adapter_down_factor[0]
    upper_matrix = adapter_up_factor[0]

    full_weight = lax.all_gather(fixed_value_weight, "dp", axis=1, tiled=True)

    picks = slot_matrix(adapter_per_token, adapter_owner_index, owners, capacity)
    both = jnp.concatenate([tokens, output_gradient], axis=1)
    outgoing = dot(picks, both, ((1,), (0,))).astype(bf16).reshape(owners, capacity, width + features)
    arrived = lax.all_to_all(outgoing, "dp", split_axis=0, concat_axis=0, tiled=True)
    arrived = arrived.reshape(slots, width + features)
    rows, grads = arrived[:, :width], arrived[:, width:]
    low = jnp.concatenate(
        [dot(rows, down_matrix, ((1,), (0,))), dot(grads, upper_matrix, ((1,), (1,)))], axis=1
    )
    own_gradient = output_gradient.reshape(slots, 2 * rank).astype(f32)
    sent = jnp.concatenate([low, own_gradient], axis=0)
    exchanged = lax.all_to_all(
        jnp.broadcast_to(sent[None], (parts,) + sent.shape), "mp", split_axis=0, concat_axis=0, tiled=True
    )
    summed = jnp.sum(exchanged[:, :slots], axis=0).astype(bf16)
    hidden, signal = summed[:, :rank], summed[:, rank:]
    whole_gradient = (
        exchanged[:, slots:].astype(bf16).reshape(parts, token_count, features).transpose(1, 0, 2)
    ).reshape(token_count, parts * features)
    extra_input = (adapter_scale * dot(signal, down_matrix, ((1,), (1,)))).astype(bf16)
    extra_output = (adapter_scale * dot(hidden, upper_matrix, ((1,), (0,)))).astype(bf16)
    back = jnp.concatenate([extra_input, extra_output], axis=1).reshape(owners, capacity, width + features)
    returned = lax.all_to_all(back, "dp", split_axis=0, concat_axis=0, tiled=True)
    returned = returned.reshape(slots, width + features)
    down_factor_gradient = adapter_scale * dot(rows, signal, ((0,), (0,)))
    up_factor_gradient = adapter_scale * dot(hidden, grads, ((0,), (0,)))

    base = dot(tokens, full_weight, ((1,), (0,)))
    base = base.reshape(token_count, parts, features).transpose(1, 0, 2)
    pieces = lax.all_to_all(base, "mp", split_axis=0, concat_axis=0, tiled=True)
    plain_input = dot(whole_gradient, full_weight, ((1,), (1,)))
    collected = dot(picks, returned, ((0,), (0,)))
    activation_gradient = (plain_input + collected[:, :width]).astype(bf16)
    projected = (jnp.sum(pieces, axis=0) + collected[:, width:]).astype(bf16)
    return (projected, activation_gradient, down_factor_gradient[None], up_factor_gradient[None])


def solution(mesh):
    return jax.shard_map(
        body,
        mesh=mesh,
        in_specs=(
            P("dp", "mp"),
            P("mp", "dp"),
            P("dp", "mp"),
            P("dp", "mp", None),
            P("dp", None, "mp"),
            P("dp", None),
            P(),
        ),
        out_specs=(P("dp", "mp"), P("dp", "mp"), P("dp", "mp", None), P("dp", None, "mp")),
        check_vma=False,
    )
```

```python
import jax
import jax.numpy as jnp
from jax import lax
from jax.experimental import pallas as pl
from jax.experimental.pallas import tpu as pltpu
from jax.sharding import PartitionSpec as P

adapter_scale = 0.5
f32 = jnp.float32
bf16 = jnp.bfloat16
VMEM_LIMIT = 48 * 1024 * 1024

N_Z, N_Y, N_C = 8, 8, 2
CLASSES = 4
FOLD = 4
CHUNK = 512


def chip_class(z, y):
    return (z + 2 * y) % CLASSES


def contract(left, right, left_dim, right_dim):
    return lax.dot_general(
        left, right, (((left_dim,), (right_dim,)), ((), ())), preferred_element_type=f32
    )


def call(kernel, outs, name, flops, nbytes, limit=VMEM_LIMIT, **kwargs):
    return pl.pallas_call(
        kernel,
        out_shape=outs,
        name=name,
        compiler_params=pltpu.CompilerParams(vmem_limit_bytes=limit),
        cost_estimate=pl.CostEstimate(flops=flops, bytes_accessed=nbytes, transcendentals=0),
        **kwargs,
    )


def paired(rows):
    return rows.reshape(rows.shape[0] // 2, 2, rows.shape[1])


def flat(pairs):
    return pairs.reshape(pairs.shape[0] * 2, pairs.shape[2])


def spread_kernel(
    adapter_hbm,
    owner_hbm,
    tokens_hbm,
    grads_hbm,
    weight_hbm,
    out_ref,
    picks_ref,
    adapter_ref,
    owner_ref,
    tokens_ref,
    grads_ref,
    weight_ref,
    sems,
):
    copies = [
        pltpu.make_async_copy(source, target, sems.at[at])
        for at, (source, target) in enumerate(
            (
                (adapter_hbm, adapter_ref),
                (owner_hbm, owner_ref),
                (weight_hbm, weight_ref),
                (grads_hbm, grads_ref),
                (tokens_hbm, tokens_ref),
            )
        )
    ]
    for copy in copies:
        copy.start()
    slots, token_count = picks_ref.shape
    adapters = owner_ref.shape[1]
    width, features = tokens_ref.shape[1], grads_ref.shape[1]
    own_features = weight_ref.shape[0]
    slices = CLASSES * N_C
    depth = width // slices

    copies[0].wait()
    copies[1].wait()
    row = lax.broadcasted_iota(jnp.int32, (slots, adapters), 0)
    owned = (owner_ref[...] == lax.shift_right_logical(row, 1)).astype(f32).astype(bf16)
    names = (
        adapter_ref[...] == lax.broadcasted_iota(jnp.int32, (adapters, token_count), 0)
    ).astype(f32).astype(bf16)
    matches = contract(owned, names, 1, 0)
    earlier = (
        lax.broadcasted_iota(jnp.int32, (token_count, token_count), 0)
        < lax.broadcasted_iota(jnp.int32, (token_count, token_count), 1)
    ).astype(f32).astype(bf16)
    before = contract(matches.astype(bf16), earlier, 1, 0)
    place = jnp.bitwise_and(lax.broadcasted_iota(jnp.int32, (slots, token_count), 0), 1).astype(f32)
    picks = jnp.where(before == place, matches, 0.0).astype(bf16)
    picks_ref[...] = picks

    copies[2].wait()
    stacked = jnp.concatenate(
        [weight_ref[:, piece * depth : (piece + 1) * depth] for piece in range(slices)], axis=0
    )
    shape = (slots, slices * own_features)
    row = lax.broadcasted_iota(jnp.int32, shape, 0)
    column = lax.broadcasted_iota(jnp.int32, shape, 1)
    device = lax.shift_right_logical(row, 1)
    z, y = lax.shift_right_logical(device, 4), jnp.bitwise_and(lax.shift_right_logical(device, 1), N_Y - 1)
    held = jnp.bitwise_and(z + 2 * y, CLASSES - 1) * N_C + jnp.bitwise_and(device, 1)
    first = held * own_features + jnp.bitwise_and(row, 1) * FOLD
    for k in range(FOLD):
        chosen = (column == first + k).astype(f32).astype(bf16)
        start = width + features + k * depth
        out_ref[:, :, start : start + depth] = paired(contract(chosen, stacked, 1, 0).astype(bf16))

    copies[3].wait()
    out_ref[:, :, width : width + features] = paired(contract(picks, grads_ref[...], 1, 0).astype(bf16))
    copies[4].wait()
    for start in range(0, width, CHUNK):
        at = pl.ds(start, CHUNK)
        out_ref[:, :, at] = paired(contract(picks, tokens_ref[:, at], 1, 0).astype(bf16))


def order_kernel(across_ref, own_ref, a_ref, b_ref, c_ref, out_ref, canonical_ref):
    parts, _, features = canonical_ref.shape
    for shift, grads_ref in enumerate((own_ref, a_ref, b_ref, c_ref)):
        canonical_ref[lax.rem(across_ref[0] + parts - shift, parts)] = grads_ref[...]
    rows = out_ref.shape[2]
    for k in range(FOLD):
        total = jnp.zeros(out_ref.shape[1:], f32)
        for block in range(parts):
            at = lax.broadcasted_iota(jnp.int32, (features, rows), 0) + block * features
            row = lax.broadcasted_iota(jnp.int32, (features, rows), 1)
            chosen = (at == FOLD * row + k).astype(f32).astype(bf16)
            total += contract(canonical_ref[block], chosen, 1, 0)
        out_ref[k] = total.astype(bf16)


def low_kernel(arrived_ref, down_ref, upper_ref, out_ref, weight_ref):
    width = down_ref.shape[1]
    features = upper_ref.shape[1]
    hidden = jnp.zeros((weight_ref.shape[0], down_ref.shape[0]), f32)
    for start in range(0, width, CHUNK):
        at = pl.ds(start, CHUNK)
        hidden += contract(flat(arrived_ref[:, :, at]), down_ref[:, at], 1, 1)
    signal = contract(flat(arrived_ref[:, :, width : width + features]), upper_ref[...], 1, 1)
    low = jnp.concatenate([hidden, signal], axis=1)
    for part in range(out_ref.shape[0]):
        out_ref[part] = low
    weight_ref[...] = flat(arrived_ref[:, :, width + features :])


def back_kernel(parts_ref, down_ref, upper_ref, low_ref, out_ref):
    rank, width = down_ref.shape
    total = parts_ref[0]
    for part in range(1, parts_ref.shape[0]):
        total = total + parts_ref[part]
    low = total.astype(bf16)
    low_ref[...] = low
    for start in range(0, width, CHUNK):
        at = pl.ds(start, CHUNK)
        out_ref[:, :, at] = paired(
            (adapter_scale * contract(low[:, rank:], down_ref[:, at], 1, 0)).astype(bf16)
        )
    out_ref[:, :, width:] = paired(
        (adapter_scale * contract(low[:, :rank], upper_ref[...], 1, 0)).astype(bf16)
    )


def factor_kernel(arrived_ref, low_ref, down_out_ref, upper_out_ref):
    rank, width = down_out_ref.shape
    features = upper_out_ref.shape[1]
    low = low_ref[...]
    for start in range(0, width, CHUNK):
        at = pl.ds(start, CHUNK)
        down_out_ref[:, at] = adapter_scale * contract(low[:, rank:], flat(arrived_ref[:, :, at]), 0, 0)
    upper_out_ref[...] = adapter_scale * contract(
        low[:, :rank], flat(arrived_ref[:, :, width : width + features]), 0, 0
    )


def finish_kernel(picks_ref, returned_ref, input_ref, own_ref, a_ref, b_ref, c_ref, out_ref, grad_ref):
    width = input_ref.shape[1]
    picks = picks_ref[...]
    for start in range(0, width, CHUNK):
        at = pl.ds(start, CHUNK)
        grad_ref[:, at] = (
            input_ref[:, at] + contract(picks, flat(returned_ref[:, :, at]), 0, 0)
        ).astype(bf16)
    base = own_ref[...] + a_ref[...] + b_ref[...] + c_ref[...]
    out_ref[...] = (base + contract(picks, flat(returned_ref[:, :, width:]), 0, 0)).astype(bf16)


def stack_kernel(*refs):
    for at, ref in enumerate(refs[:-1]):
        refs[-1][at] = ref[...]


def base_kernel(order_ref, tokens_ref, grads_ref, own_ref, other_ref, *refs):
    input_ref, *forward_refs, whole_ref = refs
    parts, _, features = whole_ref.shape
    rows, depth = own_ref.shape[1], own_ref.shape[2] // FOLD
    totals = [jnp.zeros((tokens_ref.shape[0], rows), f32) for _ in range(FOLD)]
    for step in range(2 * CLASSES):
        weight_ref = own_ref if step < CLASSES else other_ref
        at = pl.ds(pl.multiple_of(order_ref[step] * depth, depth), depth)
        part = tokens_ref[:, at]
        total = jnp.zeros((tokens_ref.shape[0], depth), f32)
        for k in range(FOLD):
            weight = weight_ref[step % CLASSES, :, k * depth : (k + 1) * depth]
            totals[k] += contract(part, weight, 1, 1)
            total += contract(grads_ref[k], weight, 1, 0)
        input_ref[:, at] = total
    for block in range(parts):
        total = jnp.zeros(whole_ref.shape[1:], f32)
        for k in range(FOLD):
            at = lax.broadcasted_iota(jnp.int32, (rows, features), 1) + block * features
            row = lax.broadcasted_iota(jnp.int32, (rows, features), 0)
            chosen = (at == FOLD * row + k).astype(f32).astype(bf16)
            rest = totals[k]
            for _ in range(3):
                term = rest.astype(bf16)
                total += contract(term, chosen, 1, 0)
                rest = rest - term.astype(f32)
        whole_ref[block] = total
    for shift, forward_ref in enumerate(forward_refs):
        forward_ref[...] = whole_ref[lax.rem(order_ref[2 * CLASSES] + shift, parts)]


def neighbour(value, dz, dy):
    pairs = []
    for z in range(N_Z):
        for y in range(N_Y):
            for core in range(N_C):
                target = ((z + dz) % N_Z) * N_Y + (y + dy) % N_Y
                pairs.append(((z * N_Y + y) * N_C + core, target * N_C + core))
    return lax.ppermute(value, "dp", pairs)


def other_core(value):
    return lax.ppermute(value, "dp", [(i, i ^ 1) for i in range(N_Z * N_Y * N_C)])


def body(
    tokens,
    fixed_value_weight,
    output_gradient,
    adapter_down_factor,
    adapter_up_factor,
    adapter_per_token,
    adapter_owner_index,
):
    owners = lax.axis_size("dp")
    parts = lax.axis_size("mp")
    token_count, width = tokens.shape
    features = output_gradient.shape[1]
    rank = adapter_down_factor.shape[2]
    adapters = adapter_owner_index.shape[0]
    capacity = 2
    slots = owners * capacity
    own_features = fixed_value_weight.shape[1]
    slices = CLASSES * N_C
    depth = width // slices
    carried = own_features * depth // capacity
    columns = width + features + carried
    all_features = owners * own_features

    me = lax.axis_index("dp")
    z, y, core = me // (N_Y * N_C), (me // N_C) % N_Y, me % N_C
    across = lax.axis_index("mp")
    down = adapter_down_factor[0].T
    upper = adapter_up_factor[0]
    hbm = pl.BlockSpec(memory_space=pltpu.HBM)
    vmem = pl.BlockSpec(memory_space=pltpu.VMEM)
    smem = pl.BlockSpec(memory_space=pltpu.SMEM)

    def around(value, shift):
        return lax.ppermute(value, "mp", [(i, (i + shift) % parts) for i in range(parts)])

    grads = [output_gradient] + [around(output_gradient, shift) for shift in range(1, parts)]

    outgoing, picks = call(
        spread_kernel,
        (
            jax.ShapeDtypeStruct((owners, capacity, columns), bf16),
            jax.ShapeDtypeStruct((slots, token_count), bf16),
        ),
        "spread",
        2 * slots * token_count * columns,
        2 * (slots + token_count) * columns,
        limit=62 * 1024 * 1024,
        in_specs=[hbm] * 5,
        out_specs=(vmem, vmem),
        scratch_shapes=[
            pltpu.VMEM((1, token_count), jnp.int32),
            pltpu.VMEM((1, adapters), jnp.int32),
            pltpu.VMEM(tokens.shape, bf16),
            pltpu.VMEM(output_gradient.shape, bf16),
            pltpu.VMEM((own_features, width), bf16),
            pltpu.SemaphoreType.DMA((5,)),
        ],
    )(
        adapter_per_token.reshape(1, token_count),
        adapter_owner_index.reshape(1, adapters),
        tokens,
        output_gradient,
        fixed_value_weight.T,
    )
    arrived = lax.all_to_all(outgoing, "dp", split_axis=0, concat_axis=0, tiled=True)
    whole_gradient = call(
        order_kernel,
        jax.ShapeDtypeStruct((FOLD, token_count, slots), bf16),
        "order",
        8 * token_count * features * slots * FOLD,
        8 * token_count * features,
        in_specs=[smem] + [vmem] * 4,
        out_specs=vmem,
        scratch_shapes=[pltpu.VMEM((parts, token_count, features), bf16)],
    )(across.reshape(1).astype(jnp.int32), *grads)
    down, upper, whole_gradient = lax.optimization_barrier((down, upper, whole_gradient))

    low_parts, weight = call(
        low_kernel,
        (
            jax.ShapeDtypeStruct((parts, slots, 2 * rank), f32),
            jax.ShapeDtypeStruct((slots, carried), bf16),
        ),
        "low_rank",
        2 * slots * rank * (width + features),
        2 * slots * columns,
    )(arrived, down, upper)
    low_parts = lax.all_to_all(low_parts, "mp", split_axis=0, concat_axis=0, tiled=True)
    near = (weight, neighbour(weight, 1, 0), neighbour(weight, -1, 0), neighbour(weight, 0, 1))

    low, back = call(
        back_kernel,
        (
            jax.ShapeDtypeStruct((slots, 2 * rank), bf16),
            jax.ShapeDtypeStruct((owners, capacity, width + features), bf16),
        ),
        "back",
        2 * slots * rank * (width + features),
        2 * slots * (width + features),
    )(low_parts, down, upper)
    returned = lax.all_to_all(back, "dp", split_axis=0, concat_axis=0, tiled=True)

    down_out, upper_out = call(
        factor_kernel,
        (
            jax.ShapeDtypeStruct((rank, width), f32),
            jax.ShapeDtypeStruct((rank, features), f32),
        ),
        "factor_gradients",
        2 * slots * rank * (width + features),
        6 * slots * (width + features),
    )(arrived, low)

    near = lax.optimization_barrier((back, near))[1]
    gathered = call(
        stack_kernel,
        jax.ShapeDtypeStruct((CLASSES, slots, carried), bf16),
        "stack",
        0,
        4 * CLASSES * slots * carried,
    )(*near)
    swapped = other_core(gathered)
    mine = chip_class(z, y)
    offsets = [0, CLASSES - 1, 1, 2]
    order = [(((mine + offset) % CLASSES) * N_C + core) for offset in offsets]
    order += [(((mine + offset) % CLASSES) * N_C + 1 - core) for offset in offsets]
    order = jnp.stack(order + [across]).astype(jnp.int32)
    plain_input, *forward = call(
        base_kernel,
        [jax.ShapeDtypeStruct((token_count, width), f32)]
        + [jax.ShapeDtypeStruct((token_count, features), f32)] * parts,
        "base",
        4 * token_count * width * all_features,
        2 * width * all_features,
        in_specs=[smem] + [vmem] * 4,
        out_specs=[vmem] * (parts + 1),
        scratch_shapes=[pltpu.VMEM((parts, token_count, features), f32)],
    )(order, tokens, whole_gradient, gathered, swapped)
    sums = [forward[0]] + [around(forward[shift], shift) for shift in range(1, parts)]

    projected, activation_gradient = call(
        finish_kernel,
        (
            jax.ShapeDtypeStruct((token_count, features), bf16),
            jax.ShapeDtypeStruct((token_count, width), bf16),
        ),
        "finish",
        2 * slots * token_count * (width + features),
        2 * slots * (width + features),
    )(picks, returned, plain_input, *sums)
    return (projected, activation_gradient, down_out.T[None], upper_out[None])


def solution(mesh):
    return jax.shard_map(
        body,
        mesh=mesh,
        in_specs=(
            P("dp", "mp"),
            P("mp", "dp"),
            P("dp", "mp"),
            P("dp", "mp", None),
            P("dp", None, "mp"),
            P("dp", None),
            P(),
        ),
        out_specs=(P("dp", "mp"), P("dp", "mp"), P("dp", "mp", None), P("dp", None, "mp")),
        check_vma=False,
    )
```

```python
import jax
import jax.numpy as jnp
from jax import lax
from jax.experimental import pallas as pl
from jax.experimental.pallas import tpu as pltpu
from jax.sharding import PartitionSpec as P

adapter_scale = 0.5
f32 = jnp.float32
bf16 = jnp.bfloat16
VMEM_LIMIT = 16 * 1024 * 1024

N_Z, N_Y, N_C = 8, 8, 2
CLASSES = 4
FOLD = 4
CHUNK = 512
WHOLE_VMEM = 62 * 1024 * 1024
LONG = 100 * 1024 * 1024


def chip_class(z, y):
    return (z + 2 * y) % CLASSES


def contract(left, right, left_dim, right_dim):
    return lax.dot_general(
        left, right, (((left_dim,), (right_dim,)), ((), ())), preferred_element_type=f32
    )


def call(kernel, outs, name, flops, nbytes, limit=VMEM_LIMIT, **kwargs):
    return pl.pallas_call(
        kernel,
        out_shape=outs,
        name=name,
        compiler_params=pltpu.CompilerParams(vmem_limit_bytes=limit),
        cost_estimate=pl.CostEstimate(flops=flops, bytes_accessed=nbytes, transcendentals=0),
        **kwargs,
    )


def paired(rows):
    return rows.reshape(rows.shape[0] // 2, 2, rows.shape[1])


def flat(pairs):
    return pairs.reshape(pairs.shape[0] * 2, pairs.shape[2])


def spread_kernel(
    adapter_hbm,
    owner_hbm,
    tokens_hbm,
    grads_hbm,
    weight_hbm,
    out_hbm,
    picks_hbm,
    out_ref,
    picks_ref,
    adapter_ref,
    owner_ref,
    tokens_ref,
    grads_ref,
    weight_ref,
    sems,
    out_sems,
):
    copies = [
        pltpu.make_async_copy(source, target, sems.at[at])
        for at, (source, target) in enumerate(
            (
                (adapter_hbm, adapter_ref),
                (owner_hbm, owner_ref),
                (weight_hbm, weight_ref),
                (grads_hbm, grads_ref),
                (tokens_hbm, tokens_ref),
            )
        )
    ]
    for copy in copies:
        copy.start()
    slots, token_count = picks_ref.shape
    adapters = owner_ref.shape[1]
    width, features = tokens_ref.shape[1], grads_ref.shape[1]
    own_features = weight_ref.shape[0]
    slices = CLASSES * N_C
    depth = width // slices

    copies[0].wait()
    copies[1].wait()
    row = lax.broadcasted_iota(jnp.int32, (slots, adapters), 0)
    owned = (owner_ref[...] == lax.shift_right_logical(row, 1)).astype(f32).astype(bf16)
    names = (
        adapter_ref[...] == lax.broadcasted_iota(jnp.int32, (adapters, token_count), 0)
    ).astype(f32).astype(bf16)
    matches = contract(owned, names, 1, 0)
    earlier = (
        lax.broadcasted_iota(jnp.int32, (token_count, token_count), 0)
        < lax.broadcasted_iota(jnp.int32, (token_count, token_count), 1)
    ).astype(f32).astype(bf16)
    before = contract(matches.astype(bf16), earlier, 1, 0)
    place = jnp.bitwise_and(lax.broadcasted_iota(jnp.int32, (slots, token_count), 0), 1).astype(f32)
    picks = jnp.where(before == place, matches, 0.0).astype(bf16)
    picks_ref[...] = picks
    stores = []

    def store(source, target):
        copy = pltpu.make_async_copy(source, target, out_sems.at[len(stores)])
        copy.start()
        stores.append(copy)

    store(picks_ref, picks_hbm)

    copies[2].wait()
    stacked = jnp.concatenate(
        [weight_ref[:, piece * depth : (piece + 1) * depth] for piece in range(slices)], axis=0
    )
    shape = (slots, slices * own_features)
    row = lax.broadcasted_iota(jnp.int32, shape, 0)
    column = lax.broadcasted_iota(jnp.int32, shape, 1)
    device = lax.shift_right_logical(row, 1)
    z, y = lax.shift_right_logical(device, 4), jnp.bitwise_and(lax.shift_right_logical(device, 1), N_Y - 1)
    held = jnp.bitwise_and(z + 2 * y, CLASSES - 1) * N_C + jnp.bitwise_and(device, 1)
    first = held * own_features + jnp.bitwise_and(row, 1) * FOLD
    for k in range(FOLD):
        chosen = (column == first + k).astype(f32).astype(bf16)
        start = width + features + k * depth
        out_ref[:, :, start : start + depth] = paired(contract(chosen, stacked, 1, 0).astype(bf16))

    at = pl.ds(width + features, out_ref.shape[2] - width - features)
    store(out_ref.at[:, :, at], out_hbm.at[:, :, at])
    copies[3].wait()
    out_ref[:, :, width : width + features] = paired(contract(picks, grads_ref[...], 1, 0).astype(bf16))
    copies[4].wait()
    for start in range(0, width, CHUNK):
        at = pl.ds(start, CHUNK)
        out_ref[:, :, at] = paired(contract(picks, tokens_ref[:, at], 1, 0).astype(bf16))
        if start + CHUNK == width:
            at = pl.ds(start, CHUNK + features)
        store(out_ref.at[:, :, at], out_hbm.at[:, :, at])
    for copy in stores:
        copy.wait()


def order_kernel(across_ref, own_ref, a_ref, b_ref, c_ref, out_ref, canonical_ref):
    parts, _, features = canonical_ref.shape
    for shift, grads_ref in enumerate((own_ref, a_ref, b_ref, c_ref)):
        canonical_ref[lax.rem(across_ref[0] + parts - shift, parts)] = grads_ref[...]
    rows = out_ref.shape[2]
    for k in range(FOLD):
        total = jnp.zeros(out_ref.shape[1:], f32)
        for block in range(parts):
            at = lax.broadcasted_iota(jnp.int32, (features, rows), 0) + block * features
            row = lax.broadcasted_iota(jnp.int32, (features, rows), 1)
            chosen = (at == FOLD * row + k).astype(f32).astype(bf16)
            total += contract(canonical_ref[block], chosen, 1, 0)
        out_ref[k] = total.astype(bf16)


def low_kernel(arrived_ref, down_ref, upper_ref, out_ref):
    width = down_ref.shape[1]
    features = upper_ref.shape[1]
    hidden = jnp.zeros((out_ref.shape[1], down_ref.shape[0]), f32)
    for start in range(0, width, CHUNK):
        at = pl.ds(start, CHUNK)
        hidden += contract(flat(arrived_ref[:, :, at]), down_ref[:, at], 1, 1)
    signal = contract(flat(arrived_ref[:, :, width : width + features]), upper_ref[...], 1, 1)
    low = jnp.concatenate([hidden, signal], axis=1)
    for part in range(out_ref.shape[0]):
        out_ref[part] = low


def weight_kernel(arrived_ref, out_ref):
    out_ref[...] = flat(arrived_ref[:, :, arrived_ref.shape[2] - out_ref.shape[1] :])


def back_kernel(parts_ref, down_ref, upper_ref, low_hbm, out_hbm, low_ref, out_ref, sems):
    rank, width = down_ref.shape
    total = parts_ref[0]
    for part in range(1, parts_ref.shape[0]):
        total = total + parts_ref[part]
    low = total.astype(bf16)
    low_ref[...] = low
    stores = [pltpu.make_async_copy(low_ref, low_hbm, sems.at[0])]
    stores[0].start()
    for start in range(0, width, CHUNK):
        at = pl.ds(start, CHUNK)
        out_ref[:, :, at] = paired(
            (adapter_scale * contract(low[:, rank:], down_ref[:, at], 1, 0)).astype(bf16)
        )
        if start + CHUNK == width:
            at = pl.ds(start, out_ref.shape[2] - start)
            out_ref[:, :, width:] = paired(
                (adapter_scale * contract(low[:, :rank], upper_ref[...], 1, 0)).astype(bf16)
            )
        stores.append(pltpu.make_async_copy(out_ref.at[:, :, at], out_hbm.at[:, :, at], sems.at[len(stores)]))
        stores[-1].start()
    for store in stores:
        store.wait()


def factor_kernel(arrived_ref, low_ref, down_out_ref, upper_out_ref):
    rank, width = down_out_ref.shape
    features = upper_out_ref.shape[1]
    low = low_ref[...]
    for start in range(0, width, CHUNK):
        at = pl.ds(start, CHUNK)
        down_out_ref[:, at] = adapter_scale * contract(low[:, rank:], flat(arrived_ref[:, :, at]), 0, 0)
    upper_out_ref[...] = adapter_scale * contract(
        low[:, :rank], flat(arrived_ref[:, :, width : width + features]), 0, 0
    )


def finish_kernel(order_ref, picks_hbm, returned_hbm, mine_hbm, other_hbm, *refs):
    *part_hbm, out_hbm, grad_hbm = refs[:-8]
    picks_ref, returned_ref, input_ref, part_ref, out_ref, grad_ref, in_sems, out_sems = refs[-8:]
    classes, _, depth = mine_hbm.shape
    width = grad_ref.shape[1]
    sources = [(picks_hbm, picks_ref)]
    for at in range(2 * classes):
        half = mine_hbm if at < classes else other_hbm
        sources.append((half.at[at % classes], input_ref.at[:, columns_of(order_ref, at, depth)]))
    early = len(sources)
    chunks = [pl.ds(start, CHUNK) for start in range(0, width, CHUNK)]
    for columns in chunks + [pl.ds(width, returned_ref.shape[2] - width)]:
        sources.append((returned_hbm.at[:, :, columns], returned_ref.at[:, :, columns]))
    for at, source in enumerate(part_hbm):
        sources.append((source, part_ref.at[at]))
    copies = [
        pltpu.make_async_copy(source, target, in_sems.at[at]) for at, (source, target) in enumerate(sources)
    ]
    for copy in copies:
        copy.start()
    for copy in copies[:early]:
        copy.wait()
    picks = picks_ref[...]
    stores = []
    for at, columns in enumerate(chunks):
        copies[early + at].wait()
        grad_ref[:, columns] = (
            input_ref[:, columns] + contract(picks, flat(returned_ref[:, :, columns]), 0, 0)
        ).astype(bf16)
        stores.append(pltpu.make_async_copy(grad_ref.at[:, columns], grad_hbm.at[:, columns], out_sems.at[at]))
        stores[-1].start()
    for copy in copies[early + len(chunks) :]:
        copy.wait()
    base = part_ref[0]
    for at in range(1, len(part_hbm)):
        base = base + part_ref[at]
    out_ref[...] = (base + contract(picks, flat(returned_ref[:, :, width:]), 0, 0)).astype(bf16)
    stores.append(pltpu.make_async_copy(out_ref, out_hbm, out_sems.at[len(chunks)]))
    stores[-1].start()
    for store in stores:
        store.wait()


def stack_kernel(*refs):
    for at, ref in enumerate(refs[:-1]):
        refs[-1][at] = ref[...]


def columns_of(order_ref, at, depth):
    return pl.ds(pl.multiple_of(order_ref[at] * depth, depth), depth)


def forward_half(order_ref, first, tokens_ref, weight_ref):
    classes, rows, carried = weight_ref.shape
    depth = carried // FOLD
    totals = [jnp.zeros((tokens_ref.shape[0], rows), f32) for _ in range(FOLD)]
    for at in range(classes):
        part = tokens_ref[:, columns_of(order_ref, first + at, depth)]
        for k in range(FOLD):
            totals[k] += contract(part, weight_ref[at, :, k * depth : (k + 1) * depth], 1, 1)
    return totals


def input_half(grads_ref, weight_ref, input_ref):
    classes, _, carried = weight_ref.shape
    depth = carried // FOLD
    for at in range(classes):
        total = contract(grads_ref[0], weight_ref[at, :, :depth], 1, 0)
        for k in range(1, FOLD):
            total += contract(grads_ref[k], weight_ref[at, :, k * depth : (k + 1) * depth], 1, 0)
        input_ref[at] = total


def own_kernel(order_ref, tokens_ref, grads_ref, weight_ref, totals_ref, input_ref):
    for k, total in enumerate(forward_half(order_ref, 0, tokens_ref, weight_ref)):
        totals_ref[k] = total
    input_half(grads_ref, weight_ref, input_ref)


def forward_kernel(order_ref, tokens_ref, totals_ref, weight_ref, *refs):
    *forward_refs, whole_ref = refs
    parts, _, features = whole_ref.shape
    totals = forward_half(order_ref, CLASSES, tokens_ref, weight_ref)
    rows = totals[0].shape[1]
    terms = []
    for k in range(FOLD):
        rest = totals[k] + totals_ref[k]
        for _ in range(3):
            terms.append((k, rest.astype(bf16)))
            rest = rest - terms[-1][1].astype(f32)
    for block in range(parts):
        at = lax.broadcasted_iota(jnp.int32, (rows, features), 1) + block * features
        row = lax.broadcasted_iota(jnp.int32, (rows, features), 0)
        total = jnp.zeros(whole_ref.shape[1:], f32)
        for k, term in terms:
            total += contract(term, (at == FOLD * row + k).astype(f32).astype(bf16), 1, 0)
        whole_ref[block] = total
    for shift, forward_ref in enumerate(forward_refs):
        forward_ref[...] = whole_ref[lax.rem(order_ref[2 * CLASSES] + shift, parts)]


def input_kernel(grads_ref, weight_ref, input_ref):
    input_half(grads_ref, weight_ref, input_ref)


def neighbour(value, dz, dy):
    pairs = []
    for z in range(N_Z):
        for y in range(N_Y):
            for core in range(N_C):
                target = ((z + dz) % N_Z) * N_Y + (y + dy) % N_Y
                pairs.append(((z * N_Y + y) * N_C + core, target * N_C + core))
    return lax.ppermute(value, "dp", pairs)


def other_core(value):
    return lax.ppermute(value, "dp", [(i, i ^ 1) for i in range(N_Z * N_Y * N_C)])


def body(
    tokens,
    fixed_value_weight,
    output_gradient,
    adapter_down_factor,
    adapter_up_factor,
    adapter_per_token,
    adapter_owner_index,
):
    owners = lax.axis_size("dp")
    parts = lax.axis_size("mp")
    token_count, width = tokens.shape
    features = output_gradient.shape[1]
    rank = adapter_down_factor.shape[2]
    adapters = adapter_owner_index.shape[0]
    capacity = 2
    slots = owners * capacity
    own_features = fixed_value_weight.shape[1]
    slices = CLASSES * N_C
    depth = width // slices
    carried = own_features * depth // capacity
    columns = width + features + carried
    all_features = owners * own_features

    me = lax.axis_index("dp")
    z, y, core = me // (N_Y * N_C), (me // N_C) % N_Y, me % N_C
    across = lax.axis_index("mp")
    down = adapter_down_factor[0].T
    upper = adapter_up_factor[0]
    hbm = pl.BlockSpec(memory_space=pltpu.HBM)
    vmem = pl.BlockSpec(memory_space=pltpu.VMEM)
    smem = pl.BlockSpec(memory_space=pltpu.SMEM)

    def around(value, shift):
        return lax.ppermute(value, "mp", [(i, (i + shift) % parts) for i in range(parts)])

    grads = [output_gradient] + [around(output_gradient, shift) for shift in range(1, parts)]

    outgoing, picks = call(
        spread_kernel,
        (
            jax.ShapeDtypeStruct((owners, capacity, columns), bf16),
            jax.ShapeDtypeStruct((slots, token_count), bf16),
        ),
        "spread",
        2 * slots * token_count * columns,
        2 * (slots + token_count) * columns,
        limit=WHOLE_VMEM,
        in_specs=[hbm] * 5,
        out_specs=(hbm, hbm),
        scratch_shapes=[
            pltpu.VMEM((owners, capacity, columns), bf16),
            pltpu.VMEM((slots, token_count), bf16),
            pltpu.VMEM((1, token_count), jnp.int32),
            pltpu.VMEM((1, adapters), jnp.int32),
            pltpu.VMEM(tokens.shape, bf16),
            pltpu.VMEM(output_gradient.shape, bf16),
            pltpu.VMEM((own_features, width), bf16),
            pltpu.SemaphoreType.DMA((5,)),
            pltpu.SemaphoreType.DMA((2 + width // CHUNK,)),
        ],
    )(
        adapter_per_token.reshape(1, token_count),
        adapter_owner_index.reshape(1, adapters),
        tokens,
        output_gradient,
        fixed_value_weight.T,
    )
    arrived = lax.all_to_all(outgoing, "dp", split_axis=0, concat_axis=0, tiled=True)
    whole_gradient = call(
        order_kernel,
        jax.ShapeDtypeStruct((FOLD, token_count, slots), bf16),
        "order",
        8 * token_count * features * slots * FOLD,
        8 * token_count * features,
        in_specs=[smem] + [vmem] * 4,
        out_specs=vmem,
        scratch_shapes=[pltpu.VMEM((parts, token_count, features), bf16)],
    )(across.reshape(1).astype(jnp.int32), *grads)
    down, upper, whole_gradient = lax.optimization_barrier((down, upper, whole_gradient))

    low_parts = call(
        low_kernel,
        jax.ShapeDtypeStruct((parts, slots, 2 * rank), f32),
        "low_rank",
        2 * slots * rank * (width + features),
        2 * slots * columns,
    )(arrived, down, upper)
    after_low = lax.optimization_barrier((low_parts, arrived))[1]
    low_parts = lax.all_to_all(low_parts, "mp", split_axis=0, concat_axis=0, tiled=True)
    weight = call(
        weight_kernel,
        jax.ShapeDtypeStruct((slots, carried), bf16),
        "weight",
        0,
        2 * slots * columns,
    )(after_low)
    near = (weight, neighbour(weight, 1, 0), neighbour(weight, -1, 0), neighbour(weight, 0, 1))

    low, back = call(
        back_kernel,
        (
            jax.ShapeDtypeStruct((slots, 2 * rank), bf16),
            jax.ShapeDtypeStruct((owners, capacity, width + features), bf16),
        ),
        "back",
        LONG * 400,
        LONG,
        out_specs=(hbm, hbm),
        scratch_shapes=[
            pltpu.VMEM((slots, 2 * rank), bf16),
            pltpu.VMEM((owners, capacity, width + features), bf16),
            pltpu.SemaphoreType.DMA((1 + width // CHUNK,)),
        ],
    )(low_parts, down, upper)
    returned = lax.all_to_all(back, "dp", split_axis=0, concat_axis=0, tiled=True)

    down_out, upper_out = call(
        factor_kernel,
        (
            jax.ShapeDtypeStruct((rank, width), f32),
            jax.ShapeDtypeStruct((rank, features), f32),
        ),
        "factor_gradients",
        LONG * 400,
        LONG,
    )(arrived, low)

    near = lax.optimization_barrier((down_out, near))[1]
    gathered = call(
        stack_kernel,
        jax.ShapeDtypeStruct((CLASSES, slots, carried), bf16),
        "stack",
        0,
        4 * CLASSES * slots * carried,
    )(*near)
    swapped = other_core(gathered)
    mine = chip_class(z, y)
    offsets = [0, CLASSES - 1, 1, 2]
    order = [(((mine + offset) % CLASSES) * N_C + core) for offset in offsets]
    order += [(((mine + offset) % CLASSES) * N_C + 1 - core) for offset in offsets]
    order = jnp.stack(order + [across]).astype(jnp.int32)
    half_work = 2 * token_count * width * all_features // 2
    by_class = jax.ShapeDtypeStruct((CLASSES, token_count, depth), f32)
    totals, own_input = call(
        own_kernel,
        (jax.ShapeDtypeStruct((FOLD, token_count, slots), f32), by_class),
        "base_own",
        2 * half_work,
        width * all_features,
        in_specs=[smem] + [vmem] * 3,
        out_specs=(vmem, vmem),
    )(order, tokens, whole_gradient, gathered)
    forward = call(
        forward_kernel,
        [jax.ShapeDtypeStruct((token_count, features), f32)] * parts,
        "base_forward",
        half_work,
        width * all_features,
        in_specs=[smem] + [vmem] * 3,
        out_specs=[vmem] * parts,
        scratch_shapes=[pltpu.VMEM((parts, token_count, features), f32)],
    )(order, tokens, totals, swapped)
    other_input = call(
        input_kernel,
        by_class,
        "base_input",
        half_work,
        width * all_features,
    )(whole_gradient, swapped)
    sums = [forward[0]] + [around(forward[shift], shift) for shift in range(1, parts)]

    projected, activation_gradient = call(
        finish_kernel,
        (
            jax.ShapeDtypeStruct((token_count, features), bf16),
            jax.ShapeDtypeStruct((token_count, width), bf16),
        ),
        "finish",
        2 * slots * token_count * (width + features),
        2 * slots * (width + features),
        limit=WHOLE_VMEM,
        in_specs=[smem] + [hbm] * (4 + parts),
        out_specs=(hbm, hbm),
        scratch_shapes=[
            pltpu.VMEM(picks.shape, bf16),
            pltpu.VMEM(returned.shape, bf16),
            pltpu.VMEM((token_count, width), f32),
            pltpu.VMEM((parts, token_count, features), f32),
            pltpu.VMEM((token_count, features), bf16),
            pltpu.VMEM((token_count, width), bf16),
            pltpu.SemaphoreType.DMA((1 + 2 * CLASSES + width // CHUNK + 1 + parts,)),
            pltpu.SemaphoreType.DMA((width // CHUNK + 1,)),
        ],
    )(order, picks, returned, own_input, other_input, *sums)
    return (projected, activation_gradient, down_out.T[None], upper_out[None])


def solution(mesh):
    return jax.shard_map(
        body,
        mesh=mesh,
        in_specs=(
            P("dp", "mp"),
            P("mp", "dp"),
            P("dp", "mp"),
            P("dp", "mp", None),
            P("dp", None, "mp"),
            P("dp", None),
            P(),
        ),
        out_specs=(P("dp", "mp"), P("dp", "mp"), P("dp", "mp", None), P("dp", None, "mp")),
        check_vma=False,
    )
```

```python
import jax
import jax.numpy as jnp
from jax import lax
from jax.experimental import pallas as pl
from jax.experimental.pallas import tpu as pltpu
from jax.sharding import PartitionSpec as P

adapter_scale = 0.5
f32 = jnp.float32
bf16 = jnp.bfloat16
VMEM_LIMIT = 16 * 1024 * 1024

N_Z, N_Y, N_C = 8, 8, 2
CLASSES = 4
FOLD = 4
CHUNK = 512
WHOLE_VMEM = 62 * 1024 * 1024
LONG = 100 * 1024 * 1024


def chip_class(z, y):
    return (z + 2 * y) % CLASSES


def contract(left, right, left_dim, right_dim):
    return lax.dot_general(
        left, right, (((left_dim,), (right_dim,)), ((), ())), preferred_element_type=f32
    )


def call(kernel, outs, name, flops, nbytes, limit=VMEM_LIMIT, **kwargs):
    return pl.pallas_call(
        kernel,
        out_shape=outs,
        name=name,
        compiler_params=pltpu.CompilerParams(vmem_limit_bytes=limit),
        cost_estimate=pl.CostEstimate(flops=flops, bytes_accessed=nbytes, transcendentals=0),
        **kwargs,
    )


def paired(rows):
    return rows.reshape(rows.shape[0] // 2, 2, rows.shape[1])


def flat(pairs):
    return pairs.reshape(pairs.shape[0] * 2, pairs.shape[2])


def spread_kernel(
    adapter_hbm,
    owner_hbm,
    tokens_hbm,
    grads_hbm,
    weight_hbm,
    out_hbm,
    picks_hbm,
    out_ref,
    picks_ref,
    adapter_ref,
    owner_ref,
    tokens_ref,
    grads_ref,
    weight_ref,
    sems,
    out_sems,
):
    copies = [
        pltpu.make_async_copy(source, target, sems.at[at])
        for at, (source, target) in enumerate(
            (
                (adapter_hbm, adapter_ref),
                (owner_hbm, owner_ref),
                (weight_hbm, weight_ref),
                (grads_hbm, grads_ref),
                (tokens_hbm, tokens_ref),
            )
        )
    ]
    for copy in copies:
        copy.start()
    slots, token_count = picks_ref.shape
    adapters = owner_ref.shape[1]
    width, features = tokens_ref.shape[1], grads_ref.shape[1]
    own_features = weight_ref.shape[0]
    slices = CLASSES * N_C
    depth = width // slices

    copies[0].wait()
    copies[1].wait()
    row = lax.broadcasted_iota(jnp.int32, (slots, adapters), 0)
    owned = (owner_ref[...] == lax.shift_right_logical(row, 1)).astype(f32).astype(bf16)
    names = (
        adapter_ref[...] == lax.broadcasted_iota(jnp.int32, (adapters, token_count), 0)
    ).astype(f32).astype(bf16)
    matches = contract(owned, names, 1, 0)
    earlier = (
        lax.broadcasted_iota(jnp.int32, (token_count, token_count), 0)
        < lax.broadcasted_iota(jnp.int32, (token_count, token_count), 1)
    ).astype(f32).astype(bf16)
    before = contract(matches.astype(bf16), earlier, 1, 0)
    place = jnp.bitwise_and(lax.broadcasted_iota(jnp.int32, (slots, token_count), 0), 1).astype(f32)
    picks = jnp.where(before == place, matches, 0.0).astype(bf16)
    picks_ref[...] = picks
    stores = []

    def store(source, target):
        copy = pltpu.make_async_copy(source, target, out_sems.at[len(stores)])
        copy.start()
        stores.append(copy)

    store(picks_ref, picks_hbm)

    copies[2].wait()
    stacked = jnp.concatenate(
        [weight_ref[:, piece * depth : (piece + 1) * depth] for piece in range(slices)], axis=0
    )
    shape = (slots, slices * own_features)
    row = lax.broadcasted_iota(jnp.int32, shape, 0)
    column = lax.broadcasted_iota(jnp.int32, shape, 1)
    device = lax.shift_right_logical(row, 1)
    z, y = lax.shift_right_logical(device, 4), jnp.bitwise_and(lax.shift_right_logical(device, 1), N_Y - 1)
    held = jnp.bitwise_and(z + 2 * y, CLASSES - 1) * N_C + jnp.bitwise_and(device, 1)
    first = held * own_features + jnp.bitwise_and(row, 1) * FOLD
    for k in range(FOLD):
        chosen = (column == first + k).astype(f32).astype(bf16)
        start = width + features + k * depth
        out_ref[:, :, start : start + depth] = paired(contract(chosen, stacked, 1, 0).astype(bf16))

    at = pl.ds(width + features, out_ref.shape[2] - width - features)
    store(out_ref.at[:, :, at], out_hbm.at[:, :, at])
    copies[3].wait()
    out_ref[:, :, width : width + features] = paired(contract(picks, grads_ref[...], 1, 0).astype(bf16))
    copies[4].wait()
    for start in range(0, width, CHUNK):
        at = pl.ds(start, CHUNK)
        out_ref[:, :, at] = paired(contract(picks, tokens_ref[:, at], 1, 0).astype(bf16))
        if start + CHUNK == width:
            at = pl.ds(start, CHUNK + features)
        store(out_ref.at[:, :, at], out_hbm.at[:, :, at])
    for copy in stores:
        copy.wait()


def order_kernel(across_ref, own_ref, a_ref, b_ref, c_ref, out_ref, canonical_ref):
    parts, _, features = canonical_ref.shape
    for shift, grads_ref in enumerate((own_ref, a_ref, b_ref, c_ref)):
        canonical_ref[lax.rem(across_ref[0] + parts - shift, parts)] = grads_ref[...]
    rows = out_ref.shape[2]
    for k in range(FOLD):
        total = jnp.zeros(out_ref.shape[1:], f32)
        for block in range(parts):
            at = lax.broadcasted_iota(jnp.int32, (features, rows), 0) + block * features
            row = lax.broadcasted_iota(jnp.int32, (features, rows), 1)
            chosen = (at == FOLD * row + k).astype(f32).astype(bf16)
            total += contract(canonical_ref[block], chosen, 1, 0)
        out_ref[k] = total.astype(bf16)


def low_kernel(arrived_ref, down_ref, upper_ref, out_ref):
    width = down_ref.shape[1]
    features = upper_ref.shape[1]
    hidden = jnp.zeros((out_ref.shape[1], down_ref.shape[0]), f32)
    for start in range(0, width, CHUNK):
        at = pl.ds(start, CHUNK)
        hidden += contract(flat(arrived_ref[:, :, at]), down_ref[:, at], 1, 1)
    signal = contract(flat(arrived_ref[:, :, width : width + features]), upper_ref[...], 1, 1)
    low = jnp.concatenate([hidden, signal], axis=1)
    for part in range(out_ref.shape[0]):
        out_ref[part] = low


def weight_kernel(arrived_ref, out_ref):
    out_ref[...] = flat(arrived_ref[:, :, arrived_ref.shape[2] - out_ref.shape[1] :])


def back_kernel(parts_ref, down_ref, upper_ref, low_hbm, out_ref, low_ref, sem):
    rank, width = down_ref.shape
    total = parts_ref[0]
    for part in range(1, parts_ref.shape[0]):
        total = total + parts_ref[part]
    low = total.astype(bf16)
    low_ref[...] = low
    store = pltpu.make_async_copy(low_ref, low_hbm, sem)
    store.start()
    for start in range(0, width, CHUNK):
        at = pl.ds(start, CHUNK)
        out_ref[:, :, at] = paired(
            (adapter_scale * contract(low[:, rank:], down_ref[:, at], 1, 0)).astype(bf16)
        )
    out_ref[:, :, width:] = paired(
        (adapter_scale * contract(low[:, :rank], upper_ref[...], 1, 0)).astype(bf16)
    )
    store.wait()


def factor_kernel(arrived_ref, low_ref, down_out_ref, upper_out_ref):
    rank, width = down_out_ref.shape
    features = upper_out_ref.shape[1]
    low = low_ref[...]
    for start in range(0, width, CHUNK):
        at = pl.ds(start, CHUNK)
        down_out_ref[:, at] = adapter_scale * contract(low[:, rank:], flat(arrived_ref[:, :, at]), 0, 0)
    upper_out_ref[...] = adapter_scale * contract(
        low[:, :rank], flat(arrived_ref[:, :, width : width + features]), 0, 0
    )


def sum_kernel(*refs):
    total = refs[0][...]
    for ref in refs[1:-1]:
        total = total + ref[...]
    refs[-1][...] = total


def finish_kernel(picks_ref, returned_ref, input_ref, base_ref, out_ref, grad_ref):
    width = input_ref.shape[1]
    picks = picks_ref[...]
    for start in range(0, width, CHUNK):
        at = pl.ds(start, CHUNK)
        grad_ref[:, at] = (
            input_ref[:, at] + contract(picks, flat(returned_ref[:, :, at]), 0, 0)
        ).astype(bf16)
    out_ref[...] = (base_ref[...] + contract(picks, flat(returned_ref[:, :, width:]), 0, 0)).astype(bf16)


def stack_kernel(*refs):
    for at, ref in enumerate(refs[:-1]):
        refs[-1][at] = ref[...]


def columns_of(order_ref, at, depth):
    return pl.ds(pl.multiple_of(order_ref[at] * depth, depth), depth)


def forward_half(order_ref, first, tokens_ref, weight_ref):
    classes, rows, carried = weight_ref.shape
    depth = carried // FOLD
    totals = [jnp.zeros((tokens_ref.shape[0], rows), f32) for _ in range(FOLD)]
    for at in range(classes):
        part = tokens_ref[:, columns_of(order_ref, first + at, depth)]
        for k in range(FOLD):
            totals[k] += contract(part, weight_ref[at, :, k * depth : (k + 1) * depth], 1, 1)
    return totals


def input_half(grads_ref, weight_ref, input_ref):
    classes, _, carried = weight_ref.shape
    depth = carried // FOLD
    for at in range(classes):
        total = contract(grads_ref[0], weight_ref[at, :, :depth], 1, 0)
        for k in range(1, FOLD):
            total += contract(grads_ref[k], weight_ref[at, :, k * depth : (k + 1) * depth], 1, 0)
        input_ref[at] = total


def own_kernel(order_ref, tokens_ref, grads_ref, weight_ref, totals_ref, input_ref):
    for k, total in enumerate(forward_half(order_ref, 0, tokens_ref, weight_ref)):
        totals_ref[k] = total
    input_half(grads_ref, weight_ref, input_ref)


def forward_kernel(order_ref, tokens_ref, totals_ref, weight_ref, *refs):
    *forward_refs, whole_ref = refs
    parts, _, features = whole_ref.shape
    totals = forward_half(order_ref, CLASSES, tokens_ref, weight_ref)
    rows = totals[0].shape[1]
    terms = []
    for k in range(FOLD):
        rest = totals[k] + totals_ref[k]
        for _ in range(3):
            terms.append((k, rest.astype(bf16)))
            rest = rest - terms[-1][1].astype(f32)
    for block in range(parts):
        at = lax.broadcasted_iota(jnp.int32, (rows, features), 1) + block * features
        row = lax.broadcasted_iota(jnp.int32, (rows, features), 0)
        total = jnp.zeros(whole_ref.shape[1:], f32)
        for k, term in terms:
            total += contract(term, (at == FOLD * row + k).astype(f32).astype(bf16), 1, 0)
        whole_ref[block] = total
    for shift, forward_ref in enumerate(forward_refs):
        forward_ref[...] = whole_ref[lax.rem(order_ref[2 * CLASSES] + shift, parts)]


def input_kernel(order_ref, grads_ref, weight_ref, own_ref, out_ref, input_ref):
    input_half(grads_ref, weight_ref, input_ref)
    depth = own_ref.shape[2]
    for at in range(CLASSES):
        out_ref[:, columns_of(order_ref, at, depth)] = own_ref[at]
        out_ref[:, columns_of(order_ref, CLASSES + at, depth)] = input_ref[at]


def neighbour(value, dz, dy):
    pairs = []
    for z in range(N_Z):
        for y in range(N_Y):
            for core in range(N_C):
                target = ((z + dz) % N_Z) * N_Y + (y + dy) % N_Y
                pairs.append(((z * N_Y + y) * N_C + core, target * N_C + core))
    return lax.ppermute(value, "dp", pairs)


def other_core(value):
    return lax.ppermute(value, "dp", [(i, i ^ 1) for i in range(N_Z * N_Y * N_C)])


def body(
    tokens,
    fixed_value_weight,
    output_gradient,
    adapter_down_factor,
    adapter_up_factor,
    adapter_per_token,
    adapter_owner_index,
):
    owners = lax.axis_size("dp")
    parts = lax.axis_size("mp")
    token_count, width = tokens.shape
    features = output_gradient.shape[1]
    rank = adapter_down_factor.shape[2]
    adapters = adapter_owner_index.shape[0]
    capacity = 2
    slots = owners * capacity
    own_features = fixed_value_weight.shape[1]
    slices = CLASSES * N_C
    depth = width // slices
    carried = own_features * depth // capacity
    columns = width + features + carried
    all_features = owners * own_features

    me = lax.axis_index("dp")
    z, y, core = me // (N_Y * N_C), (me // N_C) % N_Y, me % N_C
    across = lax.axis_index("mp")
    down = adapter_down_factor[0].T
    upper = adapter_up_factor[0]
    hbm = pl.BlockSpec(memory_space=pltpu.HBM)
    vmem = pl.BlockSpec(memory_space=pltpu.VMEM)
    smem = pl.BlockSpec(memory_space=pltpu.SMEM)

    def around(value, shift):
        return lax.ppermute(value, "mp", [(i, (i + shift) % parts) for i in range(parts)])

    grads = [output_gradient] + [around(output_gradient, shift) for shift in range(1, parts)]

    outgoing, picks = call(
        spread_kernel,
        (
            jax.ShapeDtypeStruct((owners, capacity, columns), bf16),
            jax.ShapeDtypeStruct((slots, token_count), bf16),
        ),
        "spread",
        2 * slots * token_count * columns,
        2 * (slots + token_count) * columns,
        limit=WHOLE_VMEM,
        in_specs=[hbm] * 5,
        out_specs=(hbm, hbm),
        scratch_shapes=[
            pltpu.VMEM((owners, capacity, columns), bf16),
            pltpu.VMEM((slots, token_count), bf16),
            pltpu.VMEM((1, token_count), jnp.int32),
            pltpu.VMEM((1, adapters), jnp.int32),
            pltpu.VMEM(tokens.shape, bf16),
            pltpu.VMEM(output_gradient.shape, bf16),
            pltpu.VMEM((own_features, width), bf16),
            pltpu.SemaphoreType.DMA((5,)),
            pltpu.SemaphoreType.DMA((2 + width // CHUNK,)),
        ],
    )(
        adapter_per_token.reshape(1, token_count),
        adapter_owner_index.reshape(1, adapters),
        tokens,
        output_gradient,
        fixed_value_weight.T,
    )
    arrived = lax.all_to_all(outgoing, "dp", split_axis=0, concat_axis=0, tiled=True)
    whole_gradient = call(
        order_kernel,
        jax.ShapeDtypeStruct((FOLD, token_count, slots), bf16),
        "order",
        8 * token_count * features * slots * FOLD,
        8 * token_count * features,
        in_specs=[smem] + [vmem] * 4,
        out_specs=vmem,
        scratch_shapes=[pltpu.VMEM((parts, token_count, features), bf16)],
    )(across.reshape(1).astype(jnp.int32), *grads)
    down, upper, whole_gradient = lax.optimization_barrier((down, upper, whole_gradient))

    low_parts = call(
        low_kernel,
        jax.ShapeDtypeStruct((parts, slots, 2 * rank), f32),
        "low_rank",
        2 * slots * rank * (width + features),
        2 * slots * columns,
    )(arrived, down, upper)
    after_low = lax.optimization_barrier((low_parts, arrived))[1]
    low_parts = lax.all_to_all(low_parts, "mp", split_axis=0, concat_axis=0, tiled=True)
    weight = call(
        weight_kernel,
        jax.ShapeDtypeStruct((slots, carried), bf16),
        "weight",
        0,
        2 * slots * columns,
    )(after_low)
    near = (weight, neighbour(weight, 1, 0), neighbour(weight, -1, 0), neighbour(weight, 0, 1))

    low, back = call(
        back_kernel,
        (
            jax.ShapeDtypeStruct((slots, 2 * rank), bf16),
            jax.ShapeDtypeStruct((owners, capacity, width + features), bf16),
        ),
        "back",
        LONG * 400,
        LONG,
        out_specs=(hbm, vmem),
        scratch_shapes=[pltpu.VMEM((slots, 2 * rank), bf16), pltpu.SemaphoreType.DMA],
    )(low_parts, down, upper)
    returned = lax.all_to_all(back, "dp", split_axis=0, concat_axis=0, tiled=True)

    down_out, upper_out = call(
        factor_kernel,
        (
            jax.ShapeDtypeStruct((rank, width), f32),
            jax.ShapeDtypeStruct((rank, features), f32),
        ),
        "factor_gradients",
        LONG * 400,
        LONG,
    )(arrived, low)

    near = lax.optimization_barrier((down_out, near))[1]
    gathered = call(
        stack_kernel,
        jax.ShapeDtypeStruct((CLASSES, slots, carried), bf16),
        "stack",
        0,
        4 * CLASSES * slots * carried,
    )(*near)
    swapped = other_core(gathered)
    mine = chip_class(z, y)
    offsets = [0, CLASSES - 1, 1, 2]
    order = [(((mine + offset) % CLASSES) * N_C + core) for offset in offsets]
    order += [(((mine + offset) % CLASSES) * N_C + 1 - core) for offset in offsets]
    order = jnp.stack(order + [across]).astype(jnp.int32)
    half_work = 2 * token_count * width * all_features // 2
    by_class = jax.ShapeDtypeStruct((CLASSES, token_count, depth), f32)
    totals, own_input = call(
        own_kernel,
        (jax.ShapeDtypeStruct((FOLD, token_count, slots), f32), by_class),
        "base_own",
        2 * half_work,
        width * all_features,
        in_specs=[smem] + [vmem] * 3,
        out_specs=(vmem, vmem),
    )(order, tokens, whole_gradient, gathered)
    forward = call(
        forward_kernel,
        [jax.ShapeDtypeStruct((token_count, features), f32)] * parts,
        "base_forward",
        half_work,
        width * all_features,
        in_specs=[smem] + [vmem] * 3,
        out_specs=[vmem] * parts,
        scratch_shapes=[pltpu.VMEM((parts, token_count, features), f32)],
    )(order, tokens, totals, swapped)
    plain_input = call(
        input_kernel,
        jax.ShapeDtypeStruct((token_count, width), f32),
        "base_input",
        half_work,
        width * all_features,
        in_specs=[smem] + [vmem] * 3,
        out_specs=vmem,
        scratch_shapes=[pltpu.VMEM((CLASSES, token_count, depth), f32)],
    )(order, whole_gradient, swapped, own_input)
    sums = [forward[0]] + [around(forward[shift], shift) for shift in range(1, parts)]

    plain_output = call(
        sum_kernel,
        jax.ShapeDtypeStruct((token_count, features), f32),
        "sum",
        0,
        4 * (parts + 1) * token_count * features,
    )(*sums)

    projected, activation_gradient = call(
        finish_kernel,
        (
            jax.ShapeDtypeStruct((token_count, features), bf16),
            jax.ShapeDtypeStruct((token_count, width), bf16),
        ),
        "finish",
        2 * slots * token_count * (width + features),
        2 * slots * (width + features),
        limit=WHOLE_VMEM,
    )(picks, returned, plain_input, plain_output)
    return (projected, activation_gradient, down_out.T[None], upper_out[None])


def solution(mesh):
    return jax.shard_map(
        body,
        mesh=mesh,
        in_specs=(
            P("dp", "mp"),
            P("mp", "dp"),
            P("dp", "mp"),
            P("dp", "mp", None),
            P("dp", None, "mp"),
            P("dp", None),
            P(),
        ),
        out_specs=(P("dp", "mp"), P("dp", "mp"), P("dp", "mp", None), P("dp", None, "mp")),
        check_vma=False,
    )
```

```python
import jax
import jax.numpy as jnp
from jax import lax
from jax.experimental import pallas as pl
from jax.experimental.pallas import tpu as pltpu
from jax.sharding import PartitionSpec as P

adapter_scale = 0.5
f32 = jnp.float32
bf16 = jnp.bfloat16
VMEM_LIMIT = 16 * 1024 * 1024

N_Z, N_Y, N_C = 8, 8, 2
CLASSES = 4
FOLD = 4
CHUNK = 512
WHOLE_VMEM = 62 * 1024 * 1024
LONG = 100 * 1024 * 1024


def chip_class(z, y):
    return (z + 2 * y) % CLASSES


def contract(left, right, left_dim, right_dim):
    return lax.dot_general(
        left, right, (((left_dim,), (right_dim,)), ((), ())), preferred_element_type=f32
    )


def call(kernel, outs, name, flops, nbytes, limit=VMEM_LIMIT, **kwargs):
    return pl.pallas_call(
        kernel,
        out_shape=outs,
        name=name,
        compiler_params=pltpu.CompilerParams(vmem_limit_bytes=limit),
        cost_estimate=pl.CostEstimate(flops=flops, bytes_accessed=nbytes, transcendentals=0),
        **kwargs,
    )


def paired(rows):
    return rows.reshape(rows.shape[0] // 2, 2, rows.shape[1])


def flat(pairs):
    return pairs.reshape(pairs.shape[0] * 2, pairs.shape[2])


def spread_kernel(
    adapter_hbm,
    owner_hbm,
    tokens_hbm,
    grads_hbm,
    weight_hbm,
    out_hbm,
    picks_hbm,
    out_ref,
    picks_ref,
    adapter_ref,
    owner_ref,
    tokens_ref,
    grads_ref,
    weight_ref,
    sems,
    out_sems,
):
    copies = [
        pltpu.make_async_copy(source, target, sems.at[at])
        for at, (source, target) in enumerate(
            (
                (adapter_hbm, adapter_ref),
                (owner_hbm, owner_ref),
                (weight_hbm, weight_ref),
                (grads_hbm, grads_ref),
                (tokens_hbm, tokens_ref),
            )
        )
    ]
    for copy in copies:
        copy.start()
    slots, token_count = picks_ref.shape
    adapters = owner_ref.shape[1]
    width, features = tokens_ref.shape[1], grads_ref.shape[1]
    own_features = weight_ref.shape[0]
    slices = CLASSES * N_C
    depth = width // slices

    copies[0].wait()
    copies[1].wait()
    row = lax.broadcasted_iota(jnp.int32, (slots, adapters), 0)
    owned = (owner_ref[...] == lax.shift_right_logical(row, 1)).astype(f32).astype(bf16)
    names = (
        adapter_ref[...] == lax.broadcasted_iota(jnp.int32, (adapters, token_count), 0)
    ).astype(f32).astype(bf16)
    matches = contract(owned, names, 1, 0)
    earlier = (
        lax.broadcasted_iota(jnp.int32, (token_count, token_count), 0)
        < lax.broadcasted_iota(jnp.int32, (token_count, token_count), 1)
    ).astype(f32).astype(bf16)
    before = contract(matches.astype(bf16), earlier, 1, 0)
    place = jnp.bitwise_and(lax.broadcasted_iota(jnp.int32, (slots, token_count), 0), 1).astype(f32)
    picks = jnp.where(before == place, matches, 0.0).astype(bf16)
    picks_ref[...] = picks
    stores = []

    def store(source, target):
        copy = pltpu.make_async_copy(source, target, out_sems.at[len(stores)])
        copy.start()
        stores.append(copy)

    store(picks_ref, picks_hbm)

    copies[2].wait()
    stacked = jnp.concatenate(
        [weight_ref[:, piece * depth : (piece + 1) * depth] for piece in range(slices)], axis=0
    )
    shape = (slots, slices * own_features)
    row = lax.broadcasted_iota(jnp.int32, shape, 0)
    column = lax.broadcasted_iota(jnp.int32, shape, 1)
    device = lax.shift_right_logical(row, 1)
    z, y = lax.shift_right_logical(device, 4), jnp.bitwise_and(lax.shift_right_logical(device, 1), N_Y - 1)
    held = jnp.bitwise_and(z + 2 * y, CLASSES - 1) * N_C + jnp.bitwise_and(device, 1)
    first = held * own_features + jnp.bitwise_and(row, 1) * FOLD
    for k in range(FOLD):
        chosen = (column == first + k).astype(f32).astype(bf16)
        start = width + features + k * depth
        out_ref[:, :, start : start + depth] = paired(contract(chosen, stacked, 1, 0).astype(bf16))

    at = pl.ds(width + features, out_ref.shape[2] - width - features)
    store(out_ref.at[:, :, at], out_hbm.at[:, :, at])
    copies[3].wait()
    out_ref[:, :, width : width + features] = paired(contract(picks, grads_ref[...], 1, 0).astype(bf16))
    copies[4].wait()
    for start in range(0, width, CHUNK):
        at = pl.ds(start, CHUNK)
        out_ref[:, :, at] = paired(contract(picks, tokens_ref[:, at], 1, 0).astype(bf16))
        if start + CHUNK == width:
            at = pl.ds(start, CHUNK + features)
        store(out_ref.at[:, :, at], out_hbm.at[:, :, at])
    for copy in stores:
        copy.wait()


def order_kernel(across_ref, own_ref, a_ref, b_ref, c_ref, out_ref, canonical_ref):
    parts, _, features = canonical_ref.shape
    for shift, grads_ref in enumerate((own_ref, a_ref, b_ref, c_ref)):
        canonical_ref[lax.rem(across_ref[0] + parts - shift, parts)] = grads_ref[...]
    rows = out_ref.shape[2]
    for k in range(FOLD):
        total = jnp.zeros(out_ref.shape[1:], f32)
        for block in range(parts):
            at = lax.broadcasted_iota(jnp.int32, (features, rows), 0) + block * features
            row = lax.broadcasted_iota(jnp.int32, (features, rows), 1)
            chosen = (at == FOLD * row + k).astype(f32).astype(bf16)
            total += contract(canonical_ref[block], chosen, 1, 0)
        out_ref[k] = total.astype(bf16)


def low_kernel(arrived_ref, down_ref, upper_ref, out_ref):
    width = down_ref.shape[1]
    features = upper_ref.shape[1]
    hidden = jnp.zeros((out_ref.shape[1], down_ref.shape[0]), f32)
    for start in range(0, width, CHUNK):
        at = pl.ds(start, CHUNK)
        hidden += contract(flat(arrived_ref[:, :, at]), down_ref[:, at], 1, 1)
    signal = contract(flat(arrived_ref[:, :, width : width + features]), upper_ref[...], 1, 1)
    low = jnp.concatenate([hidden, signal], axis=1)
    for part in range(out_ref.shape[0]):
        out_ref[part] = low


def weight_kernel(arrived_ref, out_ref):
    out_ref[...] = flat(arrived_ref[:, :, arrived_ref.shape[2] - out_ref.shape[1] :])


def summed(parts_ref):
    total = parts_ref[0]
    for part in range(1, parts_ref.shape[0]):
        total = total + parts_ref[part]
    return total.astype(bf16)


def back_kernel(parts_ref, down_ref, upper_ref, out_ref):
    rank, width = down_ref.shape
    low = summed(parts_ref)
    for start in range(0, width, CHUNK):
        at = pl.ds(start, CHUNK)
        out_ref[:, :, at] = paired(
            (adapter_scale * contract(low[:, rank:], down_ref[:, at], 1, 0)).astype(bf16)
        )
    out_ref[:, :, width:] = paired(
        (adapter_scale * contract(low[:, :rank], upper_ref[...], 1, 0)).astype(bf16)
    )


def factor_kernel(arrived_ref, parts_ref, down_out_ref, upper_out_ref):
    rank, width = down_out_ref.shape
    features = upper_out_ref.shape[1]
    low = summed(parts_ref)
    for start in range(0, width, CHUNK):
        at = pl.ds(start, CHUNK)
        down_out_ref[:, at] = adapter_scale * contract(low[:, rank:], flat(arrived_ref[:, :, at]), 0, 0)
    upper_out_ref[...] = adapter_scale * contract(
        low[:, :rank], flat(arrived_ref[:, :, width : width + features]), 0, 0
    )


def finish_kernel(returned_ref, ready_ref, out_ref, grad_ref):
    token_count, width = grad_ref.shape
    features = out_ref.shape[1]
    start = width + features
    picks = jnp.concatenate(
        [
            ready_ref[:, start + half * token_count : start + (half + 1) * token_count].astype(bf16)
            for half in range(2)
        ],
        axis=0,
    )
    for start in range(0, width, CHUNK):
        at = pl.ds(start, CHUNK)
        grad_ref[:, at] = (
            ready_ref[:, at] + contract(picks, flat(returned_ref[:, :, at]), 0, 0)
        ).astype(bf16)
    at = pl.ds(width, features)
    out_ref[...] = (ready_ref[:, at] + contract(picks, flat(returned_ref[:, :, at]), 0, 0)).astype(bf16)


def stack_kernel(*refs):
    for at, ref in enumerate(refs[:-1]):
        refs[-1][at] = ref[...]


def columns_of(order_ref, at, depth):
    return pl.ds(pl.multiple_of(order_ref[at] * depth, depth), depth)


def forward_half(order_ref, first, tokens_ref, weight_ref):
    classes, rows, carried = weight_ref.shape
    depth = carried // FOLD
    totals = [jnp.zeros((tokens_ref.shape[0], rows), f32) for _ in range(FOLD)]
    for at in range(classes):
        part = tokens_ref[:, columns_of(order_ref, first + at, depth)]
        for k in range(FOLD):
            totals[k] += contract(part, weight_ref[at, :, k * depth : (k + 1) * depth], 1, 1)
    return totals


def input_half(grads_ref, weight_ref, input_ref):
    classes, _, carried = weight_ref.shape
    depth = carried // FOLD
    for at in range(classes):
        total = contract(grads_ref[0], weight_ref[at, :, :depth], 1, 0)
        for k in range(1, FOLD):
            total += contract(grads_ref[k], weight_ref[at, :, k * depth : (k + 1) * depth], 1, 0)
        input_ref[at] = total


def own_kernel(order_ref, tokens_ref, grads_ref, weight_ref, totals_ref, input_ref):
    for k, total in enumerate(forward_half(order_ref, 0, tokens_ref, weight_ref)):
        totals_ref[k] = total
    input_half(grads_ref, weight_ref, input_ref)


def forward_kernel(order_ref, tokens_ref, totals_ref, weight_ref, *refs):
    *forward_refs, whole_ref = refs
    parts, _, features = whole_ref.shape
    totals = forward_half(order_ref, CLASSES, tokens_ref, weight_ref)
    rows = totals[0].shape[1]
    terms = []
    for k in range(FOLD):
        rest = totals[k] + totals_ref[k]
        for _ in range(3):
            terms.append((k, rest.astype(bf16)))
            rest = rest - terms[-1][1].astype(f32)
    for block in range(parts):
        at = lax.broadcasted_iota(jnp.int32, (rows, features), 1) + block * features
        row = lax.broadcasted_iota(jnp.int32, (rows, features), 0)
        total = jnp.zeros(whole_ref.shape[1:], f32)
        for k, term in terms:
            total += contract(term, (at == FOLD * row + k).astype(f32).astype(bf16), 1, 0)
        whole_ref[block] = total
    for shift, forward_ref in enumerate(forward_refs):
        forward_ref[...] = whole_ref[lax.rem(order_ref[2 * CLASSES] + shift, parts)]


def ready_kernel(order_ref, grads_ref, weight_ref, own_ref, picks_ref, *refs):
    *part_refs, out_ref, input_ref = refs
    input_half(grads_ref, weight_ref, input_ref)
    classes, token_count, depth = own_ref.shape
    for at in range(classes):
        out_ref[:, columns_of(order_ref, at, depth)] = own_ref[at]
        out_ref[:, columns_of(order_ref, classes + at, depth)] = input_ref[at]
    total = part_refs[0][...]
    for ref in part_refs[1:]:
        total = total + ref[...]
    start = 2 * classes * depth
    out_ref[:, start : start + total.shape[1]] = total
    start += total.shape[1]
    for half in range(2):
        rows = picks_ref[half * token_count : (half + 1) * token_count]
        out_ref[:, start + half * token_count : start + (half + 1) * token_count] = rows.astype(f32)


def neighbour(value, dz, dy):
    pairs = []
    for z in range(N_Z):
        for y in range(N_Y):
            for core in range(N_C):
                target = ((z + dz) % N_Z) * N_Y + (y + dy) % N_Y
                pairs.append(((z * N_Y + y) * N_C + core, target * N_C + core))
    return lax.ppermute(value, "dp", pairs)


def other_core(value):
    return lax.ppermute(value, "dp", [(i, i ^ 1) for i in range(N_Z * N_Y * N_C)])


def body(
    tokens,
    fixed_value_weight,
    output_gradient,
    adapter_down_factor,
    adapter_up_factor,
    adapter_per_token,
    adapter_owner_index,
):
    owners = lax.axis_size("dp")
    parts = lax.axis_size("mp")
    token_count, width = tokens.shape
    features = output_gradient.shape[1]
    rank = adapter_down_factor.shape[2]
    adapters = adapter_owner_index.shape[0]
    capacity = 2
    slots = owners * capacity
    own_features = fixed_value_weight.shape[1]
    slices = CLASSES * N_C
    depth = width // slices
    carried = own_features * depth // capacity
    columns = width + features + carried
    all_features = owners * own_features

    me = lax.axis_index("dp")
    z, y, core = me // (N_Y * N_C), (me // N_C) % N_Y, me % N_C
    across = lax.axis_index("mp")
    down = adapter_down_factor[0].T
    upper = adapter_up_factor[0]
    hbm = pl.BlockSpec(memory_space=pltpu.HBM)
    vmem = pl.BlockSpec(memory_space=pltpu.VMEM)
    smem = pl.BlockSpec(memory_space=pltpu.SMEM)

    def around(value, shift):
        return lax.ppermute(value, "mp", [(i, (i + shift) % parts) for i in range(parts)])

    grads = [output_gradient] + [around(output_gradient, shift) for shift in range(1, parts)]

    outgoing, picks = call(
        spread_kernel,
        (
            jax.ShapeDtypeStruct((owners, capacity, columns), bf16),
            jax.ShapeDtypeStruct((slots, token_count), bf16),
        ),
        "spread",
        2 * slots * token_count * columns,
        2 * (slots + token_count) * columns,
        limit=WHOLE_VMEM,
        in_specs=[hbm] * 5,
        out_specs=(hbm, hbm),
        scratch_shapes=[
            pltpu.VMEM((owners, capacity, columns), bf16),
            pltpu.VMEM((slots, token_count), bf16),
            pltpu.VMEM((1, token_count), jnp.int32),
            pltpu.VMEM((1, adapters), jnp.int32),
            pltpu.VMEM(tokens.shape, bf16),
            pltpu.VMEM(output_gradient.shape, bf16),
            pltpu.VMEM((own_features, width), bf16),
            pltpu.SemaphoreType.DMA((5,)),
            pltpu.SemaphoreType.DMA((2 + width // CHUNK,)),
        ],
    )(
        adapter_per_token.reshape(1, token_count),
        adapter_owner_index.reshape(1, adapters),
        tokens,
        output_gradient,
        fixed_value_weight.T,
    )
    arrived = lax.all_to_all(outgoing, "dp", split_axis=0, concat_axis=0, tiled=True)
    whole_gradient = call(
        order_kernel,
        jax.ShapeDtypeStruct((FOLD, token_count, slots), bf16),
        "order",
        8 * token_count * features * slots * FOLD,
        8 * token_count * features,
        in_specs=[smem] + [vmem] * 4,
        out_specs=vmem,
        scratch_shapes=[pltpu.VMEM((parts, token_count, features), bf16)],
    )(across.reshape(1).astype(jnp.int32), *grads)
    down, upper, whole_gradient = lax.optimization_barrier((down, upper, whole_gradient))

    low_parts = call(
        low_kernel,
        jax.ShapeDtypeStruct((parts, slots, 2 * rank), f32),
        "low_rank",
        2 * slots * rank * (width + features),
        2 * slots * columns,
    )(arrived, down, upper)
    after_low = lax.optimization_barrier((low_parts, arrived))[1]
    low_parts = lax.all_to_all(low_parts, "mp", split_axis=0, concat_axis=0, tiled=True)
    weight = call(
        weight_kernel,
        jax.ShapeDtypeStruct((slots, carried), bf16),
        "weight",
        0,
        2 * slots * columns,
    )(after_low)
    near = (weight, neighbour(weight, 1, 0), neighbour(weight, -1, 0), neighbour(weight, 0, 1))

    back = call(
        back_kernel,
        jax.ShapeDtypeStruct((owners, capacity, width + features), bf16),
        "back",
        LONG * 400,
        LONG,
    )(low_parts, down, upper)
    returned = lax.all_to_all(back, "dp", split_axis=0, concat_axis=0, tiled=True)

    down_out, upper_out = call(
        factor_kernel,
        (
            jax.ShapeDtypeStruct((rank, width), f32),
            jax.ShapeDtypeStruct((rank, features), f32),
        ),
        "factor_gradients",
        LONG * 400,
        LONG,
    )(arrived, low_parts)

    near = lax.optimization_barrier((down_out, near))[1]
    gathered = call(
        stack_kernel,
        jax.ShapeDtypeStruct((CLASSES, slots, carried), bf16),
        "stack",
        0,
        4 * CLASSES * slots * carried,
    )(*near)
    swapped = other_core(gathered)
    mine = chip_class(z, y)
    offsets = [0, CLASSES - 1, 1, 2]
    order = [(((mine + offset) % CLASSES) * N_C + core) for offset in offsets]
    order += [(((mine + offset) % CLASSES) * N_C + 1 - core) for offset in offsets]
    order = jnp.stack(order + [across]).astype(jnp.int32)
    half_work = 2 * token_count * width * all_features // 2
    by_class = jax.ShapeDtypeStruct((CLASSES, token_count, depth), f32)
    totals, own_input = call(
        own_kernel,
        (jax.ShapeDtypeStruct((FOLD, token_count, slots), f32), by_class),
        "base_own",
        2 * half_work,
        width * all_features,
        in_specs=[smem] + [vmem] * 3,
        out_specs=(vmem, vmem),
    )(order, tokens, whole_gradient, gathered)
    forward = call(
        forward_kernel,
        [jax.ShapeDtypeStruct((token_count, features), f32)] * parts,
        "base_forward",
        half_work,
        width * all_features,
        in_specs=[smem] + [vmem] * 3,
        out_specs=[vmem] * parts,
        scratch_shapes=[pltpu.VMEM((parts, token_count, features), f32)],
    )(order, tokens, totals, swapped)
    sums = [forward[0]] + [around(forward[shift], shift) for shift in range(1, parts)]
    ready = call(
        ready_kernel,
        jax.ShapeDtypeStruct((token_count, width + features + slots), f32),
        "ready",
        half_work,
        width * all_features,
        in_specs=[smem] + [vmem] * (4 + parts),
        out_specs=vmem,
        scratch_shapes=[pltpu.VMEM((CLASSES, token_count, depth), f32)],
    )(order, whole_gradient, swapped, own_input, picks, *sums)

    projected, activation_gradient = call(
        finish_kernel,
        (
            jax.ShapeDtypeStruct((token_count, features), bf16),
            jax.ShapeDtypeStruct((token_count, width), bf16),
        ),
        "finish",
        2 * slots * token_count * (width + features),
        2 * slots * (width + features),
    )(returned, ready)
    return (projected, activation_gradient, down_out.T[None], upper_out[None])


def solution(mesh):
    return jax.shard_map(
        body,
        mesh=mesh,
        in_specs=(
            P("dp", "mp"),
            P("mp", "dp"),
            P("dp", "mp"),
            P("dp", "mp", None),
            P("dp", None, "mp"),
            P("dp", None),
            P(),
        ),
        out_specs=(P("dp", "mp"), P("dp", "mp"), P("dp", "mp", None), P("dp", None, "mp")),
        check_vma=False,
    )
```

```python
import jax
import jax.numpy as jnp
from jax import lax
from jax.experimental import pallas as pl
from jax.experimental.pallas import tpu as pltpu
from jax.sharding import PartitionSpec as P

adapter_scale = 0.5
f32 = jnp.float32
bf16 = jnp.bfloat16
VMEM_LIMIT = 16 * 1024 * 1024

N_Z, N_Y, N_C = 8, 8, 2
CLASSES = 4
FOLD = 4
CHUNK = 512
WHOLE_VMEM = 62 * 1024 * 1024
LONG = 100 * 1024 * 1024


def chip_class(z, y):
    return (z + 2 * y) % CLASSES


def contract(left, right, left_dim, right_dim):
    return lax.dot_general(
        left, right, (((left_dim,), (right_dim,)), ((), ())), preferred_element_type=f32
    )


def call(kernel, outs, name, flops, nbytes, limit=VMEM_LIMIT, **kwargs):
    return pl.pallas_call(
        kernel,
        out_shape=outs,
        name=name,
        compiler_params=pltpu.CompilerParams(vmem_limit_bytes=limit),
        cost_estimate=pl.CostEstimate(flops=flops, bytes_accessed=nbytes, transcendentals=0),
        **kwargs,
    )


def paired(rows):
    return rows.reshape(rows.shape[0] // 2, 2, rows.shape[1])


def flat(pairs):
    return pairs.reshape(pairs.shape[0] * 2, pairs.shape[2])


def spread_kernel(
    adapter_hbm,
    owner_hbm,
    tokens_hbm,
    grads_hbm,
    weight_hbm,
    out_hbm,
    picks_hbm,
    out_ref,
    picks_ref,
    adapter_ref,
    owner_ref,
    tokens_ref,
    grads_ref,
    weight_ref,
    sems,
    out_sems,
):
    copies = [
        pltpu.make_async_copy(source, target, sems.at[at])
        for at, (source, target) in enumerate(
            (
                (adapter_hbm, adapter_ref),
                (owner_hbm, owner_ref),
                (weight_hbm, weight_ref),
                (grads_hbm, grads_ref),
                (tokens_hbm, tokens_ref),
            )
        )
    ]
    for copy in copies:
        copy.start()
    slots, token_count = picks_ref.shape
    adapters = owner_ref.shape[1]
    width, features = tokens_ref.shape[1], grads_ref.shape[1]
    own_features = weight_ref.shape[0]
    slices = CLASSES * N_C
    depth = width // slices

    copies[0].wait()
    copies[1].wait()
    row = lax.broadcasted_iota(jnp.int32, (slots, adapters), 0)
    owned = (owner_ref[...] == lax.shift_right_logical(row, 1)).astype(f32).astype(bf16)
    names = (
        adapter_ref[...] == lax.broadcasted_iota(jnp.int32, (adapters, token_count), 0)
    ).astype(f32).astype(bf16)
    matches = contract(owned, names, 1, 0)
    earlier = (
        lax.broadcasted_iota(jnp.int32, (token_count, token_count), 0)
        < lax.broadcasted_iota(jnp.int32, (token_count, token_count), 1)
    ).astype(f32).astype(bf16)
    before = contract(matches.astype(bf16), earlier, 1, 0)
    place = jnp.bitwise_and(lax.broadcasted_iota(jnp.int32, (slots, token_count), 0), 1).astype(f32)
    picks = jnp.where(before == place, matches, 0.0).astype(bf16)
    picks_ref[...] = picks
    stores = []

    def store(source, target):
        copy = pltpu.make_async_copy(source, target, out_sems.at[len(stores)])
        copy.start()
        stores.append(copy)

    store(picks_ref, picks_hbm)

    copies[2].wait()
    stacked = jnp.concatenate(
        [weight_ref[:, piece * depth : (piece + 1) * depth] for piece in range(slices)], axis=0
    )
    shape = (slots, slices * own_features)
    row = lax.broadcasted_iota(jnp.int32, shape, 0)
    column = lax.broadcasted_iota(jnp.int32, shape, 1)
    device = lax.shift_right_logical(row, 1)
    z, y = lax.shift_right_logical(device, 4), jnp.bitwise_and(lax.shift_right_logical(device, 1), N_Y - 1)
    held = jnp.bitwise_and(z + 2 * y, CLASSES - 1) * N_C + jnp.bitwise_and(device, 1)
    first = held * own_features + jnp.bitwise_and(row, 1) * FOLD
    for k in range(FOLD):
        chosen = (column == first + k).astype(f32).astype(bf16)
        start = width + features + k * depth
        out_ref[:, :, start : start + depth] = paired(contract(chosen, stacked, 1, 0).astype(bf16))

    at = pl.ds(width + features, out_ref.shape[2] - width - features)
    store(out_ref.at[:, :, at], out_hbm.at[:, :, at])
    copies[3].wait()
    out_ref[:, :, width : width + features] = paired(contract(picks, grads_ref[...], 1, 0).astype(bf16))
    copies[4].wait()
    for start in range(0, width, CHUNK):
        at = pl.ds(start, CHUNK)
        out_ref[:, :, at] = paired(contract(picks, tokens_ref[:, at], 1, 0).astype(bf16))
        if start + CHUNK == width:
            at = pl.ds(start, CHUNK + features)
        store(out_ref.at[:, :, at], out_hbm.at[:, :, at])
    for copy in stores:
        copy.wait()


def order_kernel(across_ref, own_ref, a_ref, b_ref, c_ref, out_ref, canonical_ref):
    parts, _, features = canonical_ref.shape
    for shift, grads_ref in enumerate((own_ref, a_ref, b_ref, c_ref)):
        canonical_ref[lax.rem(across_ref[0] + parts - shift, parts)] = grads_ref[...]
    rows = out_ref.shape[2]
    for k in range(FOLD):
        total = jnp.zeros(out_ref.shape[1:], f32)
        for block in range(parts):
            at = lax.broadcasted_iota(jnp.int32, (features, rows), 0) + block * features
            row = lax.broadcasted_iota(jnp.int32, (features, rows), 1)
            chosen = (at == FOLD * row + k).astype(f32).astype(bf16)
            total += contract(canonical_ref[block], chosen, 1, 0)
        out_ref[k] = total.astype(bf16)


def low_kernel(arrived_ref, down_ref, upper_ref, out_ref):
    width = down_ref.shape[1]
    features = upper_ref.shape[1]
    hidden = jnp.zeros((out_ref.shape[1], down_ref.shape[0]), f32)
    for start in range(0, width, CHUNK):
        at = pl.ds(start, CHUNK)
        hidden += contract(flat(arrived_ref[:, :, at]), down_ref[:, at], 1, 1)
    signal = contract(flat(arrived_ref[:, :, width : width + features]), upper_ref[...], 1, 1)
    low = jnp.concatenate([hidden, signal], axis=1)
    for part in range(out_ref.shape[0]):
        out_ref[part] = low


def weight_kernel(arrived_ref, out_ref):
    out_ref[...] = flat(arrived_ref[:, :, arrived_ref.shape[2] - out_ref.shape[1] :])


def summed(parts_ref):
    total = parts_ref[0]
    for part in range(1, parts_ref.shape[0]):
        total = total + parts_ref[part]
    return total.astype(bf16)


def back_kernel(parts_ref, down_ref, upper_ref, out_ref):
    rank, width = down_ref.shape
    low = summed(parts_ref)
    for start in range(0, width, CHUNK):
        at = pl.ds(start, CHUNK)
        out_ref[:, :, at] = paired(
            (adapter_scale * contract(low[:, rank:], down_ref[:, at], 1, 0)).astype(bf16)
        )
    out_ref[:, :, width:] = paired(
        (adapter_scale * contract(low[:, :rank], upper_ref[...], 1, 0)).astype(bf16)
    )


def factor_kernel(arrived_ref, parts_ref, down_out_ref, upper_out_ref):
    rank, width = down_out_ref.shape
    features = upper_out_ref.shape[1]
    low = summed(parts_ref)
    for start in range(0, width, CHUNK):
        at = pl.ds(start, CHUNK)
        down_out_ref[:, at] = adapter_scale * contract(low[:, rank:], flat(arrived_ref[:, :, at]), 0, 0)
    upper_out_ref[...] = adapter_scale * contract(
        low[:, :rank], flat(arrived_ref[:, :, width : width + features]), 0, 0
    )


def finish_kernel(returned_ref, ready_ref, out_ref, grad_ref):
    token_count, width = grad_ref.shape
    features = out_ref.shape[1]
    start = width + features
    picks = jnp.concatenate(
        [
            ready_ref[:, start + half * token_count : start + (half + 1) * token_count].astype(bf16)
            for half in range(2)
        ],
        axis=0,
    )
    for start in range(0, width, CHUNK):
        at = pl.ds(start, CHUNK)
        grad_ref[:, at] = (
            ready_ref[:, at] + contract(picks, flat(returned_ref[:, :, at]), 0, 0)
        ).astype(bf16)
    at = pl.ds(width, features)
    out_ref[...] = (ready_ref[:, at] + contract(picks, flat(returned_ref[:, :, at]), 0, 0)).astype(bf16)


def stack_kernel(*refs):
    for at, ref in enumerate(refs[:-1]):
        refs[-1][at] = ref[...]


def columns_of(order_ref, at, depth):
    return pl.ds(pl.multiple_of(order_ref[at] * depth, depth), depth)


def forward_half(order_ref, first, tokens_ref, weight_ref):
    classes, rows, carried = weight_ref.shape
    depth = carried // FOLD
    totals = [jnp.zeros((tokens_ref.shape[0], rows), f32) for _ in range(FOLD)]
    for at in range(classes):
        part = tokens_ref[:, columns_of(order_ref, first + at, depth)]
        for k in range(FOLD):
            totals[k] += contract(part, weight_ref[at, :, k * depth : (k + 1) * depth], 1, 1)
    return totals


def input_half(grads_ref, weight_ref, input_ref):
    classes, _, carried = weight_ref.shape
    depth = carried // FOLD
    for at in range(classes):
        total = contract(grads_ref[0], weight_ref[at, :, :depth], 1, 0)
        for k in range(1, FOLD):
            total += contract(grads_ref[k], weight_ref[at, :, k * depth : (k + 1) * depth], 1, 0)
        input_ref[at] = total


def own_kernel(order_ref, tokens_ref, grads_ref, weight_ref, totals_ref, input_ref):
    for k, total in enumerate(forward_half(order_ref, 0, tokens_ref, weight_ref)):
        totals_ref[k] = total
    input_half(grads_ref, weight_ref, input_ref)


def forward_kernel(order_ref, tokens_ref, totals_ref, weight_ref, *refs):
    *forward_refs, whole_ref = refs
    parts, _, features = whole_ref.shape
    totals = forward_half(order_ref, CLASSES, tokens_ref, weight_ref)
    rows = totals[0].shape[1]
    terms = []
    for k in range(FOLD):
        rest = totals[k] + totals_ref[k]
        for _ in range(3):
            terms.append((k, rest.astype(bf16)))
            rest = rest - terms[-1][1].astype(f32)
    for block in range(parts):
        at = lax.broadcasted_iota(jnp.int32, (rows, features), 1) + block * features
        row = lax.broadcasted_iota(jnp.int32, (rows, features), 0)
        total = jnp.zeros(whole_ref.shape[1:], f32)
        for k, term in terms:
            total += contract(term, (at == FOLD * row + k).astype(f32).astype(bf16), 1, 0)
        whole_ref[block] = total
    for shift, forward_ref in enumerate(forward_refs):
        forward_ref[...] = whole_ref[lax.rem(order_ref[2 * CLASSES] + shift, parts)]


def ready_kernel(order_ref, grads_ref, weight_ref, own_ref, picks_ref, *refs):
    *part_refs, out_ref, input_ref = refs
    input_half(grads_ref, weight_ref, input_ref)
    classes, token_count, depth = own_ref.shape
    for at in range(classes):
        out_ref[:, columns_of(order_ref, at, depth)] = own_ref[at]
        out_ref[:, columns_of(order_ref, classes + at, depth)] = input_ref[at]
    total = part_refs[0][...]
    for ref in part_refs[1:]:
        total = total + ref[...]
    start = 2 * classes * depth
    out_ref[:, start : start + total.shape[1]] = total
    start += total.shape[1]
    for half in range(2):
        rows = picks_ref[half * token_count : (half + 1) * token_count]
        out_ref[:, start + half * token_count : start + (half + 1) * token_count] = rows.astype(f32)


def neighbour(value, *steps):
    pairs = []
    for z in range(N_Z):
        for y in range(N_Y):
            for core in range(N_C):
                dz, dy = steps[core]
                target = ((z + dz) % N_Z) * N_Y + (y + dy) % N_Y
                pairs.append(((z * N_Y + y) * N_C + core, target * N_C + core))
    return lax.ppermute(value, "dp", pairs)


def other_core(value):
    return lax.ppermute(value, "dp", [(i, i ^ 1) for i in range(N_Z * N_Y * N_C)])


def body(
    tokens,
    fixed_value_weight,
    output_gradient,
    adapter_down_factor,
    adapter_up_factor,
    adapter_per_token,
    adapter_owner_index,
):
    owners = lax.axis_size("dp")
    parts = lax.axis_size("mp")
    token_count, width = tokens.shape
    features = output_gradient.shape[1]
    rank = adapter_down_factor.shape[2]
    adapters = adapter_owner_index.shape[0]
    capacity = 2
    slots = owners * capacity
    own_features = fixed_value_weight.shape[1]
    slices = CLASSES * N_C
    depth = width // slices
    carried = own_features * depth // capacity
    columns = width + features + carried
    all_features = owners * own_features

    me = lax.axis_index("dp")
    z, y, core = me // (N_Y * N_C), (me // N_C) % N_Y, me % N_C
    across = lax.axis_index("mp")
    down = adapter_down_factor[0].T
    upper = adapter_up_factor[0]
    hbm = pl.BlockSpec(memory_space=pltpu.HBM)
    vmem = pl.BlockSpec(memory_space=pltpu.VMEM)
    smem = pl.BlockSpec(memory_space=pltpu.SMEM)

    def around(value, shift):
        return lax.ppermute(value, "mp", [(i, (i + shift) % parts) for i in range(parts)])

    grads = [output_gradient] + [around(output_gradient, shift) for shift in range(1, parts)]

    outgoing, picks = call(
        spread_kernel,
        (
            jax.ShapeDtypeStruct((owners, capacity, columns), bf16),
            jax.ShapeDtypeStruct((slots, token_count), bf16),
        ),
        "spread",
        2 * slots * token_count * columns,
        2 * (slots + token_count) * columns,
        limit=WHOLE_VMEM,
        in_specs=[hbm] * 5,
        out_specs=(hbm, hbm),
        scratch_shapes=[
            pltpu.VMEM((owners, capacity, columns), bf16),
            pltpu.VMEM((slots, token_count), bf16),
            pltpu.VMEM((1, token_count), jnp.int32),
            pltpu.VMEM((1, adapters), jnp.int32),
            pltpu.VMEM(tokens.shape, bf16),
            pltpu.VMEM(output_gradient.shape, bf16),
            pltpu.VMEM((own_features, width), bf16),
            pltpu.SemaphoreType.DMA((5,)),
            pltpu.SemaphoreType.DMA((2 + width // CHUNK,)),
        ],
    )(
        adapter_per_token.reshape(1, token_count),
        adapter_owner_index.reshape(1, adapters),
        tokens,
        output_gradient,
        fixed_value_weight.T,
    )
    arrived = lax.all_to_all(outgoing, "dp", split_axis=0, concat_axis=0, tiled=True)
    whole_gradient = call(
        order_kernel,
        jax.ShapeDtypeStruct((FOLD, token_count, slots), bf16),
        "order",
        8 * token_count * features * slots * FOLD,
        8 * token_count * features,
        in_specs=[smem] + [vmem] * 4,
        out_specs=vmem,
        scratch_shapes=[pltpu.VMEM((parts, token_count, features), bf16)],
    )(across.reshape(1).astype(jnp.int32), *grads)
    down, upper, whole_gradient = lax.optimization_barrier((down, upper, whole_gradient))

    low_parts = call(
        low_kernel,
        jax.ShapeDtypeStruct((parts, slots, 2 * rank), f32),
        "low_rank",
        2 * slots * rank * (width + features),
        2 * slots * columns,
    )(arrived, down, upper)
    after_low = lax.optimization_barrier((low_parts, arrived))[1]
    low_parts = lax.all_to_all(low_parts, "mp", split_axis=0, concat_axis=0, tiled=True)
    weight = call(
        weight_kernel,
        jax.ShapeDtypeStruct((slots, carried), bf16),
        "weight",
        0,
        2 * slots * columns,
    )(after_low)
    near = (
        weight,
        neighbour(weight, (1, 0), (1, 0)),
        neighbour(weight, (-1, 0), (-1, 0)),
        neighbour(weight, (0, 1), (0, -1)),
    )

    back = call(
        back_kernel,
        jax.ShapeDtypeStruct((owners, capacity, width + features), bf16),
        "back",
        LONG * 400,
        LONG,
    )(low_parts, down, upper)
    returned = lax.all_to_all(back, "dp", split_axis=0, concat_axis=0, tiled=True)

    down_out, upper_out = call(
        factor_kernel,
        (
            jax.ShapeDtypeStruct((rank, width), f32),
            jax.ShapeDtypeStruct((rank, features), f32),
        ),
        "factor_gradients",
        LONG * 400,
        LONG,
    )(arrived, low_parts)

    near = lax.optimization_barrier((down_out, near))[1]
    gathered = call(
        stack_kernel,
        jax.ShapeDtypeStruct((CLASSES, slots, carried), bf16),
        "stack",
        0,
        4 * CLASSES * slots * carried,
    )(*near)
    swapped = other_core(gathered)
    mine = chip_class(z, y)
    offsets = [0, CLASSES - 1, 1, 2]
    order = [(((mine + offset) % CLASSES) * N_C + core) for offset in offsets]
    order += [(((mine + offset) % CLASSES) * N_C + 1 - core) for offset in offsets]
    order = jnp.stack(order + [across]).astype(jnp.int32)
    half_work = 2 * token_count * width * all_features // 2
    by_class = jax.ShapeDtypeStruct((CLASSES, token_count, depth), f32)
    totals, own_input = call(
        own_kernel,
        (jax.ShapeDtypeStruct((FOLD, token_count, slots), f32), by_class),
        "base_own",
        2 * half_work,
        width * all_features,
        in_specs=[smem] + [vmem] * 3,
        out_specs=(vmem, vmem),
    )(order, tokens, whole_gradient, gathered)
    forward = call(
        forward_kernel,
        [jax.ShapeDtypeStruct((token_count, features), f32)] * parts,
        "base_forward",
        half_work,
        width * all_features,
        in_specs=[smem] + [vmem] * 3,
        out_specs=[vmem] * parts,
        scratch_shapes=[pltpu.VMEM((parts, token_count, features), f32)],
    )(order, tokens, totals, swapped)
    sums = [forward[0]] + [around(forward[shift], shift) for shift in range(1, parts)]
    ready = call(
        ready_kernel,
        jax.ShapeDtypeStruct((token_count, width + features + slots), f32),
        "ready",
        half_work,
        width * all_features,
        in_specs=[smem] + [vmem] * (4 + parts),
        out_specs=vmem,
        scratch_shapes=[pltpu.VMEM((CLASSES, token_count, depth), f32)],
    )(order, whole_gradient, swapped, own_input, picks, *sums)

    projected, activation_gradient = call(
        finish_kernel,
        (
            jax.ShapeDtypeStruct((token_count, features), bf16),
            jax.ShapeDtypeStruct((token_count, width), bf16),
        ),
        "finish",
        2 * slots * token_count * (width + features),
        2 * slots * (width + features),
    )(returned, ready)
    return (projected, activation_gradient, down_out.T[None], upper_out[None])


def solution(mesh):
    return jax.shard_map(
        body,
        mesh=mesh,
        in_specs=(
            P("dp", "mp"),
            P("mp", "dp"),
            P("dp", "mp"),
            P("dp", "mp", None),
            P("dp", None, "mp"),
            P("dp", None),
            P(),
        ),
        out_specs=(P("dp", "mp"), P("dp", "mp"), P("dp", "mp", None), P("dp", None, "mp")),
        check_vma=False,
    )
```

```python
import jax
import jax.numpy as jnp
from jax import lax
from jax.experimental import pallas as pl
from jax.experimental.pallas import tpu as pltpu
from jax.sharding import PartitionSpec as P

adapter_scale = 0.5
f32 = jnp.float32
bf16 = jnp.bfloat16
VMEM_LIMIT = 16 * 1024 * 1024

N_Z, N_Y, N_C = 8, 8, 2
CLASSES = 4
FOLD = 4
CHUNK = 512
WHOLE_VMEM = 62 * 1024 * 1024
LONG = 100 * 1024 * 1024


def chip_class(z, y):
    return (z + 2 * y) % CLASSES


def contract(left, right, left_dim, right_dim):
    return lax.dot_general(
        left, right, (((left_dim,), (right_dim,)), ((), ())), preferred_element_type=f32
    )


def call(kernel, outs, name, flops, nbytes, limit=VMEM_LIMIT, **kwargs):
    return pl.pallas_call(
        kernel,
        out_shape=outs,
        name=name,
        compiler_params=pltpu.CompilerParams(vmem_limit_bytes=limit),
        cost_estimate=pl.CostEstimate(flops=flops, bytes_accessed=nbytes, transcendentals=0),
        **kwargs,
    )


def paired(rows):
    return rows.reshape(rows.shape[0] // 2, 2, rows.shape[1])


def flat(pairs):
    return pairs.reshape(pairs.shape[0] * 2, pairs.shape[2])


def spread_kernel(
    adapter_hbm,
    owner_hbm,
    tokens_hbm,
    grads_hbm,
    weight_hbm,
    out_hbm,
    picks_hbm,
    out_ref,
    picks_ref,
    adapter_ref,
    owner_ref,
    tokens_ref,
    grads_ref,
    weight_ref,
    sems,
    out_sems,
):
    copies = [
        pltpu.make_async_copy(source, target, sems.at[at])
        for at, (source, target) in enumerate(
            (
                (adapter_hbm, adapter_ref),
                (owner_hbm, owner_ref),
                (weight_hbm, weight_ref),
                (grads_hbm, grads_ref),
                (tokens_hbm, tokens_ref),
            )
        )
    ]
    for copy in copies:
        copy.start()
    slots, token_count = picks_ref.shape
    adapters = owner_ref.shape[1]
    width, features = tokens_ref.shape[1], grads_ref.shape[1]
    own_features = weight_ref.shape[0]
    slices = CLASSES * N_C
    depth = width // slices

    copies[0].wait()
    copies[1].wait()
    row = lax.broadcasted_iota(jnp.int32, (slots, adapters), 0)
    owned = (owner_ref[...] == lax.shift_right_logical(row, 1)).astype(f32).astype(bf16)
    names = (
        adapter_ref[...] == lax.broadcasted_iota(jnp.int32, (adapters, token_count), 0)
    ).astype(f32).astype(bf16)
    matches = contract(owned, names, 1, 0)
    earlier = (
        lax.broadcasted_iota(jnp.int32, (token_count, token_count), 0)
        < lax.broadcasted_iota(jnp.int32, (token_count, token_count), 1)
    ).astype(f32).astype(bf16)
    before = contract(matches.astype(bf16), earlier, 1, 0)
    place = jnp.bitwise_and(lax.broadcasted_iota(jnp.int32, (slots, token_count), 0), 1).astype(f32)
    picks = jnp.where(before == place, matches, 0.0).astype(bf16)
    picks_ref[...] = picks
    stores = []

    def store(source, target):
        copy = pltpu.make_async_copy(source, target, out_sems.at[len(stores)])
        copy.start()
        stores.append(copy)

    store(picks_ref, picks_hbm)

    copies[2].wait()
    stacked = jnp.concatenate(
        [weight_ref[:, piece * depth : (piece + 1) * depth] for piece in range(slices)], axis=0
    )
    shape = (slots, slices * own_features)
    row = lax.broadcasted_iota(jnp.int32, shape, 0)
    column = lax.broadcasted_iota(jnp.int32, shape, 1)
    device = lax.shift_right_logical(row, 1)
    z, y = lax.shift_right_logical(device, 4), jnp.bitwise_and(lax.shift_right_logical(device, 1), N_Y - 1)
    held = jnp.bitwise_and(z + 2 * y, CLASSES - 1) * N_C + jnp.bitwise_and(device, 1)
    first = held * own_features + jnp.bitwise_and(row, 1) * FOLD
    for k in range(FOLD):
        chosen = (column == first + k).astype(f32).astype(bf16)
        start = width + features + k * depth
        out_ref[:, :, start : start + depth] = paired(contract(chosen, stacked, 1, 0).astype(bf16))

    at = pl.ds(width + features, out_ref.shape[2] - width - features)
    store(out_ref.at[:, :, at], out_hbm.at[:, :, at])
    copies[3].wait()
    out_ref[:, :, width : width + features] = paired(contract(picks, grads_ref[...], 1, 0).astype(bf16))
    copies[4].wait()
    for start in range(0, width, CHUNK):
        at = pl.ds(start, CHUNK)
        out_ref[:, :, at] = paired(contract(picks, tokens_ref[:, at], 1, 0).astype(bf16))
        if start + CHUNK == width:
            at = pl.ds(start, CHUNK + features)
        store(out_ref.at[:, :, at], out_hbm.at[:, :, at])
    for copy in stores:
        copy.wait()


def order_kernel(across_ref, own_ref, a_ref, b_ref, c_ref, out_ref, canonical_ref):
    parts, _, features = canonical_ref.shape
    for shift, grads_ref in enumerate((own_ref, a_ref, b_ref, c_ref)):
        canonical_ref[lax.rem(across_ref[0] + parts - shift, parts)] = grads_ref[...]
    rows = out_ref.shape[2]
    for k in range(FOLD):
        total = jnp.zeros(out_ref.shape[1:], f32)
        for block in range(parts):
            at = lax.broadcasted_iota(jnp.int32, (features, rows), 0) + block * features
            row = lax.broadcasted_iota(jnp.int32, (features, rows), 1)
            chosen = (at == FOLD * row + k).astype(f32).astype(bf16)
            total += contract(canonical_ref[block], chosen, 1, 0)
        out_ref[k] = total.astype(bf16)


def low_kernel(arrived_ref, down_ref, upper_ref, out_ref):
    width = down_ref.shape[1]
    features = upper_ref.shape[1]
    hidden = jnp.zeros((out_ref.shape[1], down_ref.shape[0]), f32)
    for start in range(0, width, CHUNK):
        at = pl.ds(start, CHUNK)
        hidden += contract(flat(arrived_ref[:, :, at]), down_ref[:, at], 1, 1)
    signal = contract(flat(arrived_ref[:, :, width : width + features]), upper_ref[...], 1, 1)
    low = jnp.concatenate([hidden, signal], axis=1)
    for part in range(out_ref.shape[0]):
        out_ref[part] = low


def weight_kernel(arrived_ref, out_ref):
    out_ref[...] = flat(arrived_ref[:, :, arrived_ref.shape[2] - out_ref.shape[1] :])


def summed(parts_ref):
    total = parts_ref[0]
    for part in range(1, parts_ref.shape[0]):
        total = total + parts_ref[part]
    return total.astype(bf16)


def back_kernel(parts_ref, down_ref, upper_ref, out_ref):
    rank, width = down_ref.shape
    low = summed(parts_ref)
    for start in range(0, width, CHUNK):
        at = pl.ds(start, CHUNK)
        out_ref[:, :, at] = paired(
            (adapter_scale * contract(low[:, rank:], down_ref[:, at], 1, 0)).astype(bf16)
        )
    out_ref[:, :, width:] = paired(
        (adapter_scale * contract(low[:, :rank], upper_ref[...], 1, 0)).astype(bf16)
    )


def factor_kernel(arrived_ref, parts_ref, down_out_ref, upper_out_ref):
    rank, width = down_out_ref.shape
    features = upper_out_ref.shape[1]
    low = summed(parts_ref)
    for start in range(0, width, CHUNK):
        at = pl.ds(start, CHUNK)
        down_out_ref[:, at] = adapter_scale * contract(low[:, rank:], flat(arrived_ref[:, :, at]), 0, 0)
    upper_out_ref[...] = adapter_scale * contract(
        low[:, :rank], flat(arrived_ref[:, :, width : width + features]), 0, 0
    )


def finish_kernel(returned_ref, ready_ref, out_ref, grad_ref):
    token_count, width = grad_ref.shape
    features = out_ref.shape[1]
    start = width + features
    picks = jnp.concatenate(
        [
            ready_ref[:, start + half * token_count : start + (half + 1) * token_count].astype(bf16)
            for half in range(2)
        ],
        axis=0,
    )
    for start in range(0, width, CHUNK):
        at = pl.ds(start, CHUNK)
        grad_ref[:, at] = (
            ready_ref[:, at] + contract(picks, flat(returned_ref[:, :, at]), 0, 0)
        ).astype(bf16)
    at = pl.ds(width, features)
    out_ref[...] = (ready_ref[:, at] + contract(picks, flat(returned_ref[:, :, at]), 0, 0)).astype(bf16)


def stack_kernel(*refs):
    for at, ref in enumerate(refs[:-1]):
        refs[-1][at] = ref[...]


def columns_of(order_ref, at, depth):
    return pl.ds(pl.multiple_of(order_ref[at] * depth, depth), depth)


def forward_half(order_ref, first, tokens_ref, weight_ref):
    classes, rows, carried = weight_ref.shape
    depth = carried // FOLD
    totals = [jnp.zeros((tokens_ref.shape[0], rows), f32) for _ in range(FOLD)]
    for at in range(classes):
        part = tokens_ref[:, columns_of(order_ref, first + at, depth)]
        for k in range(FOLD):
            totals[k] += contract(part, weight_ref[at, :, k * depth : (k + 1) * depth], 1, 1)
    return totals


def input_half(grads_ref, weight_ref, input_ref):
    classes, _, carried = weight_ref.shape
    depth = carried // FOLD
    for at in range(classes):
        total = contract(grads_ref[0], weight_ref[at, :, :depth], 1, 0)
        for k in range(1, FOLD):
            total += contract(grads_ref[k], weight_ref[at, :, k * depth : (k + 1) * depth], 1, 0)
        input_ref[at] = total


def own_kernel(order_ref, tokens_ref, grads_ref, weight_ref, totals_ref, input_ref):
    for k, total in enumerate(forward_half(order_ref, 0, tokens_ref, weight_ref)):
        totals_ref[k] = total
    input_half(grads_ref, weight_ref, input_ref)


def forward_kernel(order_ref, tokens_ref, totals_ref, weight_ref, *refs):
    *forward_refs, whole_ref = refs
    parts, _, features = whole_ref.shape
    totals = forward_half(order_ref, CLASSES, tokens_ref, weight_ref)
    rows = totals[0].shape[1]
    terms = []
    for k in range(FOLD):
        rest = totals[k] + totals_ref[k]
        for _ in range(3):
            terms.append((k, rest.astype(bf16)))
            rest = rest - terms[-1][1].astype(f32)
    for block in range(parts):
        at = lax.broadcasted_iota(jnp.int32, (rows, features), 1) + block * features
        row = lax.broadcasted_iota(jnp.int32, (rows, features), 0)
        total = jnp.zeros(whole_ref.shape[1:], f32)
        for k, term in terms:
            total += contract(term, (at == FOLD * row + k).astype(f32).astype(bf16), 1, 0)
        whole_ref[block] = total
    for shift, forward_ref in enumerate(forward_refs):
        forward_ref[...] = whole_ref[lax.rem(order_ref[2 * CLASSES] + shift, parts)]


def ready_kernel(order_ref, grads_ref, weight_ref, own_ref, picks_ref, *refs):
    *part_refs, out_ref, input_ref = refs
    input_half(grads_ref, weight_ref, input_ref)
    classes, token_count, depth = own_ref.shape
    for at in range(classes):
        out_ref[:, columns_of(order_ref, at, depth)] = own_ref[at]
        out_ref[:, columns_of(order_ref, classes + at, depth)] = input_ref[at]
    total = part_refs[0][...]
    for ref in part_refs[1:]:
        total = total + ref[...]
    start = 2 * classes * depth
    out_ref[:, start : start + total.shape[1]] = total
    start += total.shape[1]
    for half in range(2):
        rows = picks_ref[half * token_count : (half + 1) * token_count]
        out_ref[:, start + half * token_count : start + (half + 1) * token_count] = rows.astype(f32)


def neighbour(value, *steps):
    pairs = []
    for z in range(N_Z):
        for y in range(N_Y):
            for core in range(N_C):
                dz, dy = steps[core]
                target = ((z + dz) % N_Z) * N_Y + (y + dy) % N_Y
                pairs.append(((z * N_Y + y) * N_C + core, target * N_C + core))
    return lax.ppermute(value, "dp", pairs)


def other_core(value):
    return lax.ppermute(value, "dp", [(i, i ^ 1) for i in range(N_Z * N_Y * N_C)])


def body(
    tokens,
    fixed_value_weight,
    output_gradient,
    adapter_down_factor,
    adapter_up_factor,
    adapter_per_token,
    adapter_owner_index,
):
    owners = lax.axis_size("dp")
    parts = lax.axis_size("mp")
    token_count, width = tokens.shape
    features = output_gradient.shape[1]
    rank = adapter_down_factor.shape[2]
    adapters = adapter_owner_index.shape[0]
    capacity = 2
    slots = owners * capacity
    own_features = fixed_value_weight.shape[1]
    slices = CLASSES * N_C
    depth = width // slices
    carried = own_features * depth // capacity
    columns = width + features + carried
    all_features = owners * own_features

    me = lax.axis_index("dp")
    z, y, core = me // (N_Y * N_C), (me // N_C) % N_Y, me % N_C
    across = lax.axis_index("mp")
    down = adapter_down_factor[0].T
    upper = adapter_up_factor[0]
    hbm = pl.BlockSpec(memory_space=pltpu.HBM)
    vmem = pl.BlockSpec(memory_space=pltpu.VMEM)
    smem = pl.BlockSpec(memory_space=pltpu.SMEM)

    def around(value, shift):
        return lax.ppermute(value, "mp", [(i, (i + shift) % parts) for i in range(parts)])

    grads = [output_gradient] + [around(output_gradient, shift) for shift in range(1, parts)]

    outgoing, picks = call(
        spread_kernel,
        (
            jax.ShapeDtypeStruct((owners, capacity, columns), bf16),
            jax.ShapeDtypeStruct((slots, token_count), bf16),
        ),
        "spread",
        2 * slots * token_count * columns,
        2 * (slots + token_count) * columns,
        limit=WHOLE_VMEM,
        in_specs=[hbm] * 5,
        out_specs=(hbm, hbm),
        scratch_shapes=[
            pltpu.VMEM((owners, capacity, columns), bf16),
            pltpu.VMEM((slots, token_count), bf16),
            pltpu.VMEM((1, token_count), jnp.int32),
            pltpu.VMEM((1, adapters), jnp.int32),
            pltpu.VMEM(tokens.shape, bf16),
            pltpu.VMEM(output_gradient.shape, bf16),
            pltpu.VMEM((own_features, width), bf16),
            pltpu.SemaphoreType.DMA((5,)),
            pltpu.SemaphoreType.DMA((2 + width // CHUNK,)),
        ],
    )(
        adapter_per_token.reshape(1, token_count),
        adapter_owner_index.reshape(1, adapters),
        tokens,
        output_gradient,
        fixed_value_weight.T,
    )
    arrived = lax.all_to_all(outgoing, "dp", split_axis=0, concat_axis=0, tiled=True)
    whole_gradient = call(
        order_kernel,
        jax.ShapeDtypeStruct((FOLD, token_count, slots), bf16),
        "order",
        8 * token_count * features * slots * FOLD,
        8 * token_count * features,
        in_specs=[smem] + [vmem] * 4,
        out_specs=vmem,
        scratch_shapes=[pltpu.VMEM((parts, token_count, features), bf16)],
    )(across.reshape(1).astype(jnp.int32), *grads)
    down, upper, whole_gradient = lax.optimization_barrier((down, upper, whole_gradient))

    low_parts = call(
        low_kernel,
        jax.ShapeDtypeStruct((parts, slots, 2 * rank), f32),
        "low_rank",
        2 * slots * rank * (width + features),
        2 * slots * columns,
    )(arrived, down, upper)
    after_low = lax.optimization_barrier((low_parts, arrived))[1]
    low_parts = lax.all_to_all(low_parts, "mp", split_axis=0, concat_axis=0, tiled=True)
    weight = call(
        weight_kernel,
        jax.ShapeDtypeStruct((slots, carried), bf16),
        "weight",
        0,
        2 * slots * columns,
    )(after_low)
    near = (
        weight,
        neighbour(weight, (0, 1), (0, -1)),
        neighbour(weight, (-1, 0), (-1, 0)),
        neighbour(weight, (1, 0), (1, 0)),
    )

    back = call(
        back_kernel,
        jax.ShapeDtypeStruct((owners, capacity, width + features), bf16),
        "back",
        LONG * 400,
        LONG,
    )(low_parts, down, upper)
    returned = lax.all_to_all(back, "dp", split_axis=0, concat_axis=0, tiled=True)

    down_out, upper_out = call(
        factor_kernel,
        (
            jax.ShapeDtypeStruct((rank, width), f32),
            jax.ShapeDtypeStruct((rank, features), f32),
        ),
        "factor_gradients",
        LONG * 400,
        LONG,
    )(arrived, low_parts)

    near = lax.optimization_barrier((down_out, near))[1]
    gathered = call(
        stack_kernel,
        jax.ShapeDtypeStruct((CLASSES, slots, carried), bf16),
        "stack",
        0,
        4 * CLASSES * slots * carried,
    )(*near)
    swapped = other_core(gathered)
    mine = chip_class(z, y)
    offsets = [0, 2, 1, CLASSES - 1]
    order = [(((mine + offset) % CLASSES) * N_C + core) for offset in offsets]
    order += [(((mine + offset) % CLASSES) * N_C + 1 - core) for offset in offsets]
    order = jnp.stack(order + [across]).astype(jnp.int32)
    half_work = 2 * token_count * width * all_features // 2
    by_class = jax.ShapeDtypeStruct((CLASSES, token_count, depth), f32)
    totals, own_input = call(
        own_kernel,
        (jax.ShapeDtypeStruct((FOLD, token_count, slots), f32), by_class),
        "base_own",
        2 * half_work,
        width * all_features,
        in_specs=[smem] + [vmem] * 3,
        out_specs=(vmem, vmem),
    )(order, tokens, whole_gradient, gathered)
    forward = call(
        forward_kernel,
        [jax.ShapeDtypeStruct((token_count, features), f32)] * parts,
        "base_forward",
        half_work,
        width * all_features,
        in_specs=[smem] + [vmem] * 3,
        out_specs=[vmem] * parts,
        scratch_shapes=[pltpu.VMEM((parts, token_count, features), f32)],
    )(order, tokens, totals, swapped)
    sums = [forward[0]] + [around(forward[shift], shift) for shift in range(1, parts)]
    ready = call(
        ready_kernel,
        jax.ShapeDtypeStruct((token_count, width + features + slots), f32),
        "ready",
        half_work,
        width * all_features,
        in_specs=[smem] + [vmem] * (4 + parts),
        out_specs=vmem,
        scratch_shapes=[pltpu.VMEM((CLASSES, token_count, depth), f32)],
    )(order, whole_gradient, swapped, own_input, picks, *sums)

    projected, activation_gradient = call(
        finish_kernel,
        (
            jax.ShapeDtypeStruct((token_count, features), bf16),
            jax.ShapeDtypeStruct((token_count, width), bf16),
        ),
        "finish",
        2 * slots * token_count * (width + features),
        2 * slots * (width + features),
    )(returned, ready)
    return (projected, activation_gradient, down_out.T[None], upper_out[None])


def solution(mesh):
    return jax.shard_map(
        body,
        mesh=mesh,
        in_specs=(
            P("dp", "mp"),
            P("mp", "dp"),
            P("dp", "mp"),
            P("dp", "mp", None),
            P("dp", None, "mp"),
            P("dp", None),
            P(),
        ),
        out_specs=(P("dp", "mp"), P("dp", "mp"), P("dp", "mp", None), P("dp", None, "mp")),
        check_vma=False,
    )
```

```python
import jax
import jax.numpy as jnp
from jax import lax
from jax.experimental import pallas as pl
from jax.experimental.pallas import tpu as pltpu
from jax.sharding import PartitionSpec as P

adapter_scale = 0.5
f32 = jnp.float32
bf16 = jnp.bfloat16
VMEM_LIMIT = 16 * 1024 * 1024

N_Z, N_Y, N_C = 8, 8, 2
CLASSES = 4
FOLD = 4
CHUNK = 512
WHOLE_VMEM = 62 * 1024 * 1024
LONG = 100 * 1024 * 1024


def chip_class(z, y):
    return (z + 2 * y) % CLASSES


def contract(left, right, left_dim, right_dim):
    return lax.dot_general(
        left, right, (((left_dim,), (right_dim,)), ((), ())), preferred_element_type=f32
    )


def call(kernel, outs, name, flops, nbytes, limit=VMEM_LIMIT, **kwargs):
    return pl.pallas_call(
        kernel,
        out_shape=outs,
        name=name,
        compiler_params=pltpu.CompilerParams(vmem_limit_bytes=limit),
        cost_estimate=pl.CostEstimate(flops=flops, bytes_accessed=nbytes, transcendentals=0),
        **kwargs,
    )


def paired(rows):
    return rows.reshape(rows.shape[0] // 2, 2, rows.shape[1])


def flat(pairs):
    return pairs.reshape(pairs.shape[0] * 2, pairs.shape[2])


def spread_kernel(
    adapter_hbm,
    owner_hbm,
    tokens_hbm,
    grads_hbm,
    weight_hbm,
    out_hbm,
    picks_hbm,
    out_ref,
    picks_ref,
    adapter_ref,
    owner_ref,
    tokens_ref,
    grads_ref,
    weight_ref,
    sems,
    out_sems,
):
    copies = [
        pltpu.make_async_copy(source, target, sems.at[at])
        for at, (source, target) in enumerate(
            (
                (adapter_hbm, adapter_ref),
                (owner_hbm, owner_ref),
                (weight_hbm, weight_ref),
                (grads_hbm, grads_ref),
                (tokens_hbm, tokens_ref),
            )
        )
    ]
    for copy in copies:
        copy.start()
    slots, token_count = picks_ref.shape
    adapters = owner_ref.shape[1]
    width, features = tokens_ref.shape[1], grads_ref.shape[1]
    own_features = weight_ref.shape[0]
    slices = CLASSES * N_C
    depth = width // slices

    copies[0].wait()
    copies[1].wait()
    row = lax.broadcasted_iota(jnp.int32, (slots, adapters), 0)
    owned = (owner_ref[...] == lax.shift_right_logical(row, 1)).astype(f32).astype(bf16)
    names = (
        adapter_ref[...] == lax.broadcasted_iota(jnp.int32, (adapters, token_count), 0)
    ).astype(f32).astype(bf16)
    matches = contract(owned, names, 1, 0)
    earlier = (
        lax.broadcasted_iota(jnp.int32, (token_count, token_count), 0)
        < lax.broadcasted_iota(jnp.int32, (token_count, token_count), 1)
    ).astype(f32).astype(bf16)
    before = contract(matches.astype(bf16), earlier, 1, 0)
    place = jnp.bitwise_and(lax.broadcasted_iota(jnp.int32, (slots, token_count), 0), 1).astype(f32)
    picks = jnp.where(before == place, matches, 0.0).astype(bf16)
    picks_ref[...] = picks
    stores = []

    def store(source, target):
        copy = pltpu.make_async_copy(source, target, out_sems.at[len(stores)])
        copy.start()
        stores.append(copy)

    store(picks_ref, picks_hbm)

    copies[2].wait()
    stacked = jnp.concatenate(
        [weight_ref[:, piece * depth : (piece + 1) * depth] for piece in range(slices)], axis=0
    )
    shape = (slots, slices * own_features)
    row = lax.broadcasted_iota(jnp.int32, shape, 0)
    column = lax.broadcasted_iota(jnp.int32, shape, 1)
    device = lax.shift_right_logical(row, 1)
    z, y = lax.shift_right_logical(device, 4), jnp.bitwise_and(lax.shift_right_logical(device, 1), N_Y - 1)
    held = jnp.bitwise_and(z + 2 * y, CLASSES - 1) * N_C + jnp.bitwise_and(device, 1)
    first = held * own_features + jnp.bitwise_and(row, 1) * FOLD
    for k in range(FOLD):
        chosen = (column == first + k).astype(f32).astype(bf16)
        start = width + features + k * depth
        out_ref[:, :, start : start + depth] = paired(contract(chosen, stacked, 1, 0).astype(bf16))

    at = pl.ds(width + features, out_ref.shape[2] - width - features)
    store(out_ref.at[:, :, at], out_hbm.at[:, :, at])
    copies[3].wait()
    out_ref[:, :, width : width + features] = paired(contract(picks, grads_ref[...], 1, 0).astype(bf16))
    copies[4].wait()
    for start in range(0, width, CHUNK):
        at = pl.ds(start, CHUNK)
        out_ref[:, :, at] = paired(contract(picks, tokens_ref[:, at], 1, 0).astype(bf16))
        if start + CHUNK == width:
            at = pl.ds(start, CHUNK + features)
        store(out_ref.at[:, :, at], out_hbm.at[:, :, at])
    for copy in stores:
        copy.wait()


def order_kernel(across_ref, own_ref, a_ref, b_ref, c_ref, out_ref, canonical_ref):
    parts, _, features = canonical_ref.shape
    for shift, grads_ref in enumerate((own_ref, a_ref, b_ref, c_ref)):
        canonical_ref[lax.rem(across_ref[0] + parts - shift, parts)] = grads_ref[...]
    rows = out_ref.shape[2]
    for k in range(FOLD):
        total = jnp.zeros(out_ref.shape[1:], f32)
        for block in range(parts):
            at = lax.broadcasted_iota(jnp.int32, (features, rows), 0) + block * features
            row = lax.broadcasted_iota(jnp.int32, (features, rows), 1)
            chosen = (at == FOLD * row + k).astype(f32).astype(bf16)
            total += contract(canonical_ref[block], chosen, 1, 0)
        out_ref[k] = total.astype(bf16)


def low_kernel(arrived_ref, down_ref, upper_ref, out_ref):
    width = down_ref.shape[1]
    features = upper_ref.shape[1]
    hidden = jnp.zeros((out_ref.shape[1], down_ref.shape[0]), f32)
    for start in range(0, width, CHUNK):
        at = pl.ds(start, CHUNK)
        hidden += contract(flat(arrived_ref[:, :, at]), down_ref[:, at], 1, 1)
    signal = contract(flat(arrived_ref[:, :, width : width + features]), upper_ref[...], 1, 1)
    low = jnp.concatenate([hidden, signal], axis=1)
    for part in range(out_ref.shape[0]):
        out_ref[part] = low


def weight_kernel(arrived_ref, out_ref):
    out_ref[...] = flat(arrived_ref[:, :, arrived_ref.shape[2] - out_ref.shape[1] :])


def summed(parts_ref):
    total = parts_ref[0]
    for part in range(1, parts_ref.shape[0]):
        total = total + parts_ref[part]
    return total.astype(bf16)


def back_kernel(parts_ref, down_ref, upper_ref, out_ref):
    rank, width = down_ref.shape
    low = summed(parts_ref)
    for start in range(0, width, CHUNK):
        at = pl.ds(start, CHUNK)
        out_ref[:, :, at] = paired(
            (adapter_scale * contract(low[:, rank:], down_ref[:, at], 1, 0)).astype(bf16)
        )
    out_ref[:, :, width:] = paired(
        (adapter_scale * contract(low[:, :rank], upper_ref[...], 1, 0)).astype(bf16)
    )


def factor_kernel(arrived_ref, parts_ref, down_out_ref, upper_out_ref):
    rank, width = down_out_ref.shape
    features = upper_out_ref.shape[1]
    low = summed(parts_ref)
    for start in range(0, width, CHUNK):
        at = pl.ds(start, CHUNK)
        down_out_ref[:, at] = adapter_scale * contract(low[:, rank:], flat(arrived_ref[:, :, at]), 0, 0)
    upper_out_ref[...] = adapter_scale * contract(
        low[:, :rank], flat(arrived_ref[:, :, width : width + features]), 0, 0
    )


def finish_kernel(returned_ref, ready_ref, out_ref, grad_ref):
    token_count, width = grad_ref.shape
    features = out_ref.shape[1]
    start = width + features
    picks = jnp.concatenate(
        [
            ready_ref[:, start + half * token_count : start + (half + 1) * token_count].astype(bf16)
            for half in range(2)
        ],
        axis=0,
    )
    for start in range(0, width, CHUNK):
        at = pl.ds(start, CHUNK)
        grad_ref[:, at] = (
            ready_ref[:, at] + contract(picks, flat(returned_ref[:, :, at]), 0, 0)
        ).astype(bf16)
    at = pl.ds(width, features)
    out_ref[...] = (ready_ref[:, at] + contract(picks, flat(returned_ref[:, :, at]), 0, 0)).astype(bf16)


def stack_kernel(*refs):
    for at, ref in enumerate(refs[:-1]):
        refs[-1][at] = ref[...]


def columns_of(order_ref, at, depth):
    return pl.ds(pl.multiple_of(order_ref[at] * depth, depth), depth)


def forward_half(order_ref, first, tokens_ref, weight_ref):
    classes, rows, carried = weight_ref.shape
    depth = carried // FOLD
    totals = [jnp.zeros((tokens_ref.shape[0], rows), f32) for _ in range(FOLD)]
    for at in range(classes):
        part = tokens_ref[:, columns_of(order_ref, first + at, depth)]
        for k in range(FOLD):
            totals[k] += contract(part, weight_ref[at, :, k * depth : (k + 1) * depth], 1, 1)
    return totals


def input_half(grads_ref, weight_ref, input_ref):
    classes, _, carried = weight_ref.shape
    depth = carried // FOLD
    for at in range(classes):
        total = contract(grads_ref[0], weight_ref[at, :, :depth], 1, 0)
        for k in range(1, FOLD):
            total += contract(grads_ref[k], weight_ref[at, :, k * depth : (k + 1) * depth], 1, 0)
        input_ref[at] = total


def own_kernel(order_ref, tokens_ref, grads_ref, weight_ref, totals_ref, input_ref):
    for k, total in enumerate(forward_half(order_ref, 0, tokens_ref, weight_ref)):
        totals_ref[k] = total
    input_half(grads_ref, weight_ref, input_ref)


def forward_kernel(order_ref, tokens_ref, totals_ref, weight_ref, *refs):
    *forward_refs, whole_ref = refs
    parts, _, features = whole_ref.shape
    totals = forward_half(order_ref, CLASSES, tokens_ref, weight_ref)
    rows = totals[0].shape[1]
    terms = []
    for k in range(FOLD):
        rest = totals[k] + totals_ref[k]
        for _ in range(3):
            terms.append((k, rest.astype(bf16)))
            rest = rest - terms[-1][1].astype(f32)
    for block in range(parts):
        at = lax.broadcasted_iota(jnp.int32, (rows, features), 1) + block * features
        row = lax.broadcasted_iota(jnp.int32, (rows, features), 0)
        total = jnp.zeros(whole_ref.shape[1:], f32)
        for k, term in terms:
            total += contract(term, (at == FOLD * row + k).astype(f32).astype(bf16), 1, 0)
        whole_ref[block] = total
    for shift, forward_ref in enumerate(forward_refs):
        forward_ref[...] = whole_ref[lax.rem(order_ref[2 * CLASSES] + shift, parts)]


def ready_kernel(order_ref, grads_ref, weight_ref, own_ref, picks_ref, *refs):
    *part_refs, out_ref, input_ref = refs
    input_half(grads_ref, weight_ref, input_ref)
    classes, token_count, depth = own_ref.shape
    for at in range(classes):
        out_ref[:, columns_of(order_ref, at, depth)] = own_ref[at]
        out_ref[:, columns_of(order_ref, classes + at, depth)] = input_ref[at]
    total = part_refs[0][...]
    for ref in part_refs[1:]:
        total = total + ref[...]
    start = 2 * classes * depth
    out_ref[:, start : start + total.shape[1]] = total
    start += total.shape[1]
    for half in range(2):
        rows = picks_ref[half * token_count : (half + 1) * token_count]
        out_ref[:, start + half * token_count : start + (half + 1) * token_count] = rows.astype(f32)


def neighbour(value, *steps):
    pairs = []
    for z in range(N_Z):
        for y in range(N_Y):
            for core in range(N_C):
                dz, dy = steps[core]
                target = ((z + dz) % N_Z) * N_Y + (y + dy) % N_Y
                pairs.append(((z * N_Y + y) * N_C + core, target * N_C + core))
    return lax.ppermute(value, "dp", pairs)


def other_core(value):
    return lax.ppermute(value, "dp", [(i, i ^ 1) for i in range(N_Z * N_Y * N_C)])


def body(
    tokens,
    fixed_value_weight,
    output_gradient,
    adapter_down_factor,
    adapter_up_factor,
    adapter_per_token,
    adapter_owner_index,
):
    owners = lax.axis_size("dp")
    parts = lax.axis_size("mp")
    token_count, width = tokens.shape
    features = output_gradient.shape[1]
    rank = adapter_down_factor.shape[2]
    adapters = adapter_owner_index.shape[0]
    capacity = 2
    slots = owners * capacity
    own_features = fixed_value_weight.shape[1]
    slices = CLASSES * N_C
    depth = width // slices
    carried = own_features * depth // capacity
    columns = width + features + carried
    all_features = owners * own_features

    me = lax.axis_index("dp")
    z, y, core = me // (N_Y * N_C), (me // N_C) % N_Y, me % N_C
    across = lax.axis_index("mp")
    down = adapter_down_factor[0].T
    upper = adapter_up_factor[0]
    hbm = pl.BlockSpec(memory_space=pltpu.HBM)
    vmem = pl.BlockSpec(memory_space=pltpu.VMEM)
    smem = pl.BlockSpec(memory_space=pltpu.SMEM)

    def around(value, shift):
        return lax.ppermute(value, "mp", [(i, (i + shift) % parts) for i in range(parts)])

    grads = [output_gradient] + [around(output_gradient, shift) for shift in range(1, parts)]

    outgoing, picks = call(
        spread_kernel,
        (
            jax.ShapeDtypeStruct((owners, capacity, columns), bf16),
            jax.ShapeDtypeStruct((slots, token_count), bf16),
        ),
        "spread",
        2 * slots * token_count * columns,
        2 * (slots + token_count) * columns,
        limit=WHOLE_VMEM,
        in_specs=[hbm] * 5,
        out_specs=(hbm, hbm),
        scratch_shapes=[
            pltpu.VMEM((owners, capacity, columns), bf16),
            pltpu.VMEM((slots, token_count), bf16),
            pltpu.VMEM((1, token_count), jnp.int32),
            pltpu.VMEM((1, adapters), jnp.int32),
            pltpu.VMEM(tokens.shape, bf16),
            pltpu.VMEM(output_gradient.shape, bf16),
            pltpu.VMEM((own_features, width), bf16),
            pltpu.SemaphoreType.DMA((5,)),
            pltpu.SemaphoreType.DMA((2 + width // CHUNK,)),
        ],
    )(
        adapter_per_token.reshape(1, token_count),
        adapter_owner_index.reshape(1, adapters),
        tokens,
        output_gradient,
        fixed_value_weight.T,
    )
    arrived = lax.all_to_all(outgoing, "dp", split_axis=0, concat_axis=0, tiled=True)
    whole_gradient = call(
        order_kernel,
        jax.ShapeDtypeStruct((FOLD, token_count, slots), bf16),
        "order",
        8 * token_count * features * slots * FOLD,
        8 * token_count * features,
        in_specs=[smem] + [vmem] * 4,
        out_specs=vmem,
        scratch_shapes=[pltpu.VMEM((parts, token_count, features), bf16)],
    )(across.reshape(1).astype(jnp.int32), *grads)
    down, upper, whole_gradient = lax.optimization_barrier((down, upper, whole_gradient))

    low_parts = call(
        low_kernel,
        jax.ShapeDtypeStruct((parts, slots, 2 * rank), f32),
        "low_rank",
        2 * slots * rank * (width + features),
        2 * slots * columns,
    )(arrived, down, upper)
    after_low = lax.optimization_barrier((low_parts, arrived))[1]
    low_parts = lax.all_to_all(low_parts, "mp", split_axis=0, concat_axis=0, tiled=True)
    weight = call(
        weight_kernel,
        jax.ShapeDtypeStruct((slots, carried), bf16),
        "weight",
        0,
        2 * slots * columns,
    )(after_low)
    near = (
        weight,
        neighbour(weight, (0, 1), (0, -1)),
        neighbour(weight, (1, 0), (1, 0)),
        neighbour(weight, (-1, 0), (-1, 0)),
    )

    back = call(
        back_kernel,
        jax.ShapeDtypeStruct((owners, capacity, width + features), bf16),
        "back",
        LONG * 400,
        LONG,
    )(low_parts, down, upper)
    returned = lax.all_to_all(back, "dp", split_axis=0, concat_axis=0, tiled=True)

    down_out, upper_out = call(
        factor_kernel,
        (
            jax.ShapeDtypeStruct((rank, width), f32),
            jax.ShapeDtypeStruct((rank, features), f32),
        ),
        "factor_gradients",
        LONG * 400,
        LONG,
    )(arrived, low_parts)

    near = lax.optimization_barrier((down_out, near))[1]
    gathered = call(
        stack_kernel,
        jax.ShapeDtypeStruct((CLASSES, slots, carried), bf16),
        "stack",
        0,
        4 * CLASSES * slots * carried,
    )(*near)
    swapped = other_core(gathered)
    mine = chip_class(z, y)
    offsets = [0, 2, CLASSES - 1, 1]
    order = [(((mine + offset) % CLASSES) * N_C + core) for offset in offsets]
    order += [(((mine + offset) % CLASSES) * N_C + 1 - core) for offset in offsets]
    order = jnp.stack(order + [across]).astype(jnp.int32)
    half_work = 2 * token_count * width * all_features // 2
    by_class = jax.ShapeDtypeStruct((CLASSES, token_count, depth), f32)
    totals, own_input = call(
        own_kernel,
        (jax.ShapeDtypeStruct((FOLD, token_count, slots), f32), by_class),
        "base_own",
        2 * half_work,
        width * all_features,
        in_specs=[smem] + [vmem] * 3,
        out_specs=(vmem, vmem),
    )(order, tokens, whole_gradient, gathered)
    forward = call(
        forward_kernel,
        [jax.ShapeDtypeStruct((token_count, features), f32)] * parts,
        "base_forward",
        half_work,
        width * all_features,
        in_specs=[smem] + [vmem] * 3,
        out_specs=[vmem] * parts,
        scratch_shapes=[pltpu.VMEM((parts, token_count, features), f32)],
    )(order, tokens, totals, swapped)
    sums = [forward[0]] + [around(forward[shift], shift) for shift in range(1, parts)]
    ready = call(
        ready_kernel,
        jax.ShapeDtypeStruct((token_count, width + features + slots), f32),
        "ready",
        half_work,
        width * all_features,
        in_specs=[smem] + [vmem] * (4 + parts),
        out_specs=vmem,
        scratch_shapes=[pltpu.VMEM((CLASSES, token_count, depth), f32)],
    )(order, whole_gradient, swapped, own_input, picks, *sums)

    projected, activation_gradient = call(
        finish_kernel,
        (
            jax.ShapeDtypeStruct((token_count, features), bf16),
            jax.ShapeDtypeStruct((token_count, width), bf16),
        ),
        "finish",
        2 * slots * token_count * (width + features),
        2 * slots * (width + features),
    )(returned, ready)
    return (projected, activation_gradient, down_out.T[None], upper_out[None])


def solution(mesh):
    return jax.shard_map(
        body,
        mesh=mesh,
        in_specs=(
            P("dp", "mp"),
            P("mp", "dp"),
            P("dp", "mp"),
            P("dp", "mp", None),
            P("dp", None, "mp"),
            P("dp", None),
            P(),
        ),
        out_specs=(P("dp", "mp"), P("dp", "mp"), P("dp", "mp", None), P("dp", None, "mp")),
        check_vma=False,
    )
```
